1024 devices in a mesh: blk: 64 (over x, z_lo, core), grp: 16 (over y, z_hi).
Axes of the slice: x: 8, y: 8, z: 8 (z_hi: 2, z_lo: 4; z = z_hi * 4 + z_lo), core: 2. Of those that a mesh axis runs over, the one named last changes fastest.
Arguments:
- node_feats: float32 [131072, 256], P(('blk', 'grp')), may hold values from -6 to 6
- dest_block: int32 [1024, 24], P(('blk', 'grp')), may hold values from 0 to 63, as said below
- col_tile: int32 [1024, 24], P(('blk', 'grp')), may hold values from 0 to 15
- tile_count: int32 [1024], P(('blk', 'grp')), may hold values from 1 to 24, as said below
- edge_tiles: bfloat16 [1024, 24, 128, 128], P(('blk', 'grp')), as said below
- w_self: bfloat16 [256, 256], replicated, may hold values from -0.375 to 0.375
- w_agg: bfloat16 [256, 256], replicated, may hold values from -0.375 to 0.375
- in_bias: float32 [256], replicated, may hold values from -3 to 3
- w_out: bfloat16 [256, 256], replicated, may hold values from -0.375 to 0.375
- out_gain: float32 [256], replicated, may hold values from 0.5 to 2
- grad_out: float32 [131072, 256], P(('blk', 'grp')), may hold values from -6 to 6
Outputs:
- updated: float32 [131072, 256], P(('blk', 'grp'))
- grad_x: float32 [131072, 256], P(('blk', 'grp'))
- tile_grads: bfloat16 [1024, 24, 128, 128], P(('blk', 'grp'))
The draws below stay inside these ranges and needn't reach their ends.
Inputs may be any that keep to these rules, and one draw needn't show every extreme that they name: dest_block[s,t] lies at most 3 steps from the shard's own block s // 16 on the closed loop of 64 blocks; within one shard's row the slots name pairwise different (dest_block, col_tile) pairs. `tile_count`: in every draw some shard has all 24 slots live. `edge_tiles`: most entries are zero.
All inputs are finite; a program needn't handle non-finite values.
Results may differ from the reference program's by a relative error of at most 0.01.
Values may be sent and summed in bfloat16 or wider, within the bound.
A program may use at most 32 MiB of HBM per device.

```python
import math
import jax
import jax.numpy as jnp
from jax import lax

FEAT = 256
TILE = 128
HALO = 3
TILES_DEV = 24
ROWS_DEV = 128
COLT = 16
SHARDS = 1024
NODES = 131072
N_BLK = 64
N_GRP = 16


def slot_pairs(key):
    base = jax.random.fold_in(key, 11)
    combos = (2 * HALO + 1) * COLT
    shard_keys = jax.random.split(base, SHARDS)
    centre = (jnp.arange(combos) // COLT == HALO).astype(jnp.int32)

    def pick_slots(one_key):
        scores = jax.random.randint(one_key, (combos,), 0, 1024) + 256 * centre
        distinct = scores * combos + jnp.arange(combos).astype(jnp.int32)
        return lax.top_k(distinct, TILES_DEV)[1]
    return jax.vmap(pick_slots)(shard_keys).astype(jnp.int32)


def draw_dest_block(key, part):
    relative = slot_pairs(key) // COLT - HALO
    own_block = (jnp.arange(SHARDS) // N_GRP)[:, None]
    return ((own_block + relative) % N_BLK).astype(jnp.int32)


def draw_col_tile(key, part):
    return (slot_pairs(key) % COLT).astype(jnp.int32)


def draw_tile_count(key, part):
    base = jax.random.fold_in(key, 23)
    spread = jax.random.randint(base, (SHARDS,), 0, TILES_DEV)
    counts = 1 + spread * spread // TILES_DEV
    full_shard = jax.random.randint(jax.random.fold_in(base, 1), (), 0, SHARDS)
    counts = jnp.where(jnp.arange(SHARDS) == full_shard, TILES_DEV, counts)
    return counts.astype(jnp.int32)


def draw_edge_tiles(key, part):
    shape = (SHARDS, TILES_DEV, ROWS_DEV, TILE)
    keep = jax.random.uniform(jax.random.fold_in(key, 31), shape) < 2.0 / TILE
    factor = (2.0 * (TILES_DEV / 3.0 + 1.0)) ** (-0.5)
    values = jax.random.normal(jax.random.fold_in(key, 37), shape) * factor
    return jnp.where(keep, values, 0.0).astype(jnp.bfloat16)


def block_levels(key, shape, pieces, smallest, top_value):
    gain = 1.0
    for dim, parts in pieces:
        draws = jax.random.uniform(jax.random.fold_in(jax.random.fold_in(key, 6), dim), (parts,), jnp.float32, smallest / len(pieces), top_value / len(pieces))
        gain = gain * jnp.repeat(jnp.exp(draws), shape[dim] // parts).reshape((-1,) + (1,) * (len(shape) - 1 - dim))
    return gain


def bell_draw(rng, dims, deviation, most, shards=(), kind=jnp.bfloat16):
    entries = deviation * jax.random.normal(rng, dims, jnp.float32)
    if shards:
        entries = entries * block_levels(rng, dims, shards, -0.22, 0.18)
    return jnp.clip(entries, -most, most).astype(kind)


def setup_inputs(seed: int = 0) -> dict:
    seeds = jax.random.split(jax.random.key(seed), 12)
    node_feats = bell_draw(seeds[0], (NODES, FEAT), 1.0, 6.0, ((0, 1024),), jnp.float32)
    dest_block = draw_dest_block(jax.random.fold_in(seeds[11], 71), 0)
    col_tile = draw_col_tile(jax.random.fold_in(seeds[11], 71), 0)
    tile_count = draw_tile_count(jax.random.fold_in(seeds[11], 71), 0)
    edge_tiles = draw_edge_tiles(jax.random.fold_in(seeds[11], 71), 0)
    w_self = bell_draw(seeds[5], (FEAT, FEAT), FEAT ** -0.5, 0.375)
    w_agg = bell_draw(seeds[6], (FEAT, FEAT), FEAT ** -0.5, 0.375)
    in_bias = bell_draw(seeds[7], (FEAT,), 0.5, 3.0, (), jnp.float32)
    w_out = bell_draw(seeds[8], (FEAT, FEAT), FEAT ** -0.5, 0.375)
    out_gain = jnp.clip(jnp.exp(jax.random.uniform(seeds[9], (FEAT,), jnp.float32, math.log(0.5), math.log(2.0))), 0.5, 2.0)
    grad_out = bell_draw(seeds[10], (NODES, FEAT), 1.0, 6.0, ((0, 1024),), jnp.float32)
    return dict(node_feats=node_feats, dest_block=dest_block, col_tile=col_tile, tile_count=tile_count, edge_tiles=edge_tiles, w_self=w_self, w_agg=w_agg, in_bias=in_bias, w_out=w_out, out_gain=out_gain, grad_out=grad_out)


ln_eps = 1e-05

def node_forward(node_feats, feat_bf, agg_bf, w_self, w_agg, in_bias, w_out, out_gain):
    pre_act = jnp.dot(feat_bf, w_self, preferred_element_type=jnp.float32) + jnp.dot(agg_bf, w_agg, preferred_element_type=jnp.float32) + in_bias
    hidden = jax.nn.silu(pre_act).astype(jnp.bfloat16)
    mixed = jnp.dot(hidden, w_out, preferred_element_type=jnp.float32)
    centred = mixed - lax.optimization_barrier(jnp.mean(mixed, axis=-1, keepdims=True))
    variance = lax.optimization_barrier(jnp.mean(centred * centred, axis=-1, keepdims=True))
    inv_std = lax.rsqrt(variance + ln_eps)
    normed = centred * inv_std
    return (node_feats + out_gain * normed, pre_act, normed, inv_std)

def node_backward(grad_out, pre_act, normed, inv_std, w_self, w_agg, w_out, out_gain):
    g_norm = grad_out * out_gain
    g_mixed = inv_std * (g_norm - lax.optimization_barrier(jnp.mean(g_norm, axis=-1, keepdims=True)) - normed * lax.optimization_barrier(jnp.mean(g_norm * normed, axis=-1, keepdims=True)))
    g_mixed = g_mixed.astype(jnp.bfloat16)
    g_hidden = jnp.dot(g_mixed, w_out.T, preferred_element_type=jnp.float32)
    sigmoid_z = jax.nn.sigmoid(pre_act)
    g_pre = (g_hidden * sigmoid_z * (1.0 + pre_act * (1.0 - sigmoid_z))).astype(jnp.bfloat16)
    own_grad = jnp.dot(g_pre, w_self.T, preferred_element_type=jnp.float32)
    agg_grad = jnp.dot(g_pre, w_agg.T, preferred_element_type=jnp.float32).astype(jnp.bfloat16)
    return (own_grad, agg_grad)

def reference(node_feats, dest_block, col_tile, tile_count, edge_tiles, w_self, w_agg, in_bias, w_out, out_gain, grad_out):
    feat_bf = node_feats.astype(jnp.bfloat16)
    feat_blocks = feat_bf.reshape(N_BLK, COLT, TILE, FEAT)
    top_precision = lax.Precision.HIGHEST

    def shard_parts(shard):
        blk_idx = shard // N_GRP
        live_slot = (jnp.arange(TILES_DEV) < tile_count[shard]).astype(jnp.float32)
        edge_weights = edge_tiles[shard].astype(jnp.float32) * live_slot[:, None, None]
        column_features = feat_blocks[blk_idx][col_tile[shard]].astype(jnp.float32)
        return (blk_idx, live_slot, edge_weights, column_features)

    def forward_step(aggregate, shard):
        grp_idx = shard % N_GRP
        blk_idx, live_slot, edge_weights, column_features = shard_parts(shard)
        weighted_products = jnp.einsum('jcx,jxv->jcv', edge_weights, column_features, precision=top_precision)
        return (aggregate.at[dest_block[shard], grp_idx].add(weighted_products), None)
    shard_ids = jnp.arange(SHARDS).astype(jnp.int32)
    start = jnp.zeros((N_BLK, N_GRP, ROWS_DEV, FEAT), jnp.float32)
    aggregate, unused = lax.scan(forward_step, start, shard_ids)
    agg_bf = aggregate.reshape(NODES, FEAT).astype(jnp.bfloat16)
    updated, pre_act, normed, inv_std = node_forward(node_feats, feat_bf, agg_bf, w_self, w_agg, in_bias, w_out, out_gain)
    own_grad, agg_grad = node_backward(grad_out, pre_act, normed, inv_std, w_self, w_agg, w_out, out_gain)
    grad_blocks = agg_grad.reshape(N_BLK, N_GRP, ROWS_DEV, FEAT)

    def backward_step(source_grad, shard):
        grp_idx = shard % N_GRP
        blk_idx, live_slot, edge_weights, column_features = shard_parts(shard)
        target_gradients = grad_blocks[dest_block[shard], grp_idx].astype(jnp.float32)
        tile_gradient = jnp.einsum('lme,lae->lma', target_gradients, column_features, precision=top_precision)
        tile_gradient = (tile_gradient * live_slot[:, None, None]).astype(jnp.bfloat16)
        tile_message_terms = jnp.einsum('ghx,ghv->gxv', edge_weights, target_gradients, precision=top_precision)
        return (source_grad.at[blk_idx, col_tile[shard]].add(tile_message_terms), tile_gradient)
    start_grad = jnp.zeros((N_BLK, COLT, TILE, FEAT), jnp.float32)
    source_grad, tile_grads = lax.scan(backward_step, start_grad, shard_ids)
    grad_x = grad_out + own_grad + source_grad.reshape(NODES, FEAT)
    return (updated, grad_x, tile_grads)
```

```python
import jax
import jax.numpy as jnp
from jax import lax
from jax.experimental import pallas as pl
from jax.experimental.pallas import tpu as pltpu
from jax.sharding import PartitionSpec as P

HALO = 3
SPAN = 2 * HALO + 1
LN_EPS = 1e-05
BF16 = jnp.bfloat16
F32 = jnp.float32


def matmul(left, right):
    return jnp.dot(left, right, preferred_element_type=F32)


def matmul_nt(left, right):
    return lax.dot_general(left, right, (((1,), (1,)), ((), ())), preferred_element_type=F32)


def kernel(
    dest_ref,
    col_ref,
    count_ref,
    feats_hbm,
    edge_hbm,
    w_self_hbm,
    w_agg_hbm,
    bias_hbm,
    w_out_hbm,
    gain_hbm,
    grad_hbm,
    updated_hbm,
    grad_x_hbm,
    tile_grads_hbm,
    feats,
    edge,
    w_self,
    w_agg,
    bias,
    w_out,
    gain,
    grad,
    updated,
    grad_x,
    tile_grads,
    table_v,
    table,
    edge_t,
    dense,
    dense_t,
    gathered,
    part_out,
    part_in,
    near,
    red_out,
    red_in,
    swap_out,
    swap_in,
    pre_base,
    own_grad,
    local_sems,
    out_sems,
    table_sem,
    ring_send,
    ring_recv,
    pair_send,
    pair_recv,
    part_send,
    part_recv,
    near_send,
    near_recv,
    red_send,
    red_recv,
    swap_send,
    swap_recv,
):
    rows = feats.shape[0]
    half = feats.shape[1] // 2
    slots = edge.shape[0] - 1
    members = gathered.shape[1]
    ring = members // 2
    reach = ring // 2
    blocks = lax.axis_size("blk")
    blk = lax.axis_index("blk")
    grp = lax.axis_index("grp")
    ring_at = grp // 2
    plane = grp % 2

    def member(ring_pos, q):
        return lax.rem(ring_pos + 2 * ring, ring) * 2 + (plane if q == 0 else 1 - plane)

    def to_ring(direction):
        return {"grp": member(ring_at + (1 if direction == 0 else -1), 0)}

    def to_pair():
        return {"grp": member(ring_at, 1)}

    def to_blk(offset):
        return {"blk": lax.rem(blk + offset + blocks, blocks)}

    offsets = [o for o in range(-HALO, HALO + 1) if o != 0]

    loads = [
        pltpu.make_async_copy(src, dst, local_sems.at[i])
        for i, (src, dst) in enumerate(
            [
                (feats_hbm, feats),
                (edge_hbm.at[0], edge.at[pl.ds(0, slots)]),
                (w_self_hbm, w_self),
                (bias_hbm, bias),
                (w_agg_hbm, w_agg),
                (w_out_hbm, w_out),
                (gain_hbm, gain),
                (grad_hbm, grad),
            ]
        )
    ]
    for load in loads:
        load.start()

    barrier = pltpu.get_barrier_semaphore()
    greeted = [to_ring(0), to_ring(1), to_pair()] + [to_blk(o) for o in offsets]
    for target in greeted:
        pl.semaphore_signal(barrier, inc=1, device_id=target, device_id_type=pl.DeviceIdType.MESH)

    lane = lax.broadcasted_iota(jnp.int32, table_v.shape, 1)
    found = jnp.full(table_v.shape, slots, jnp.int32)
    for t in range(slots):
        rel = lax.rem(dest_ref[0, t] - blk + HALO + blocks, blocks)
        key = jnp.where(t < count_ref[0], rel * members + col_ref[0, t], -1)
        found = jnp.where(lane == key, t, found)
    table_v[...] = found
    table_copy = pltpu.make_async_copy(table_v, table, table_sem)
    table_copy.start()

    loads[0].wait()
    feat_bf = feats[...].astype(BF16)
    mine = member(ring_at, 0)
    for h in range(2):
        gathered[h, mine] = feat_bf[:, h * half : (h + 1) * half]

    pl.semaphore_wait(barrier, len(greeted))

    def ring_id(h, q, direction, step):
        return ((h * 2 + q) * 2 + direction) * reach + step - 1

    def in_flow(q, direction, step):
        return step < reach or q == direction

    def ring_copy(h, q, direction, step, incoming=False):
        back = step if incoming else step - 1
        at = member(ring_at + (-back if direction == 0 else back), q)
        i = ring_id(h, q, direction, step)
        return pltpu.make_async_remote_copy(
            src_ref=gathered.at[h, at],
            dst_ref=gathered.at[h, at],
            send_sem=ring_send.at[i],
            recv_sem=ring_recv.at[i],
            device_id=to_ring(direction),
            device_id_type=pl.DeviceIdType.MESH,
        )

    def pair_copy(h, incoming=False):
        at = member(ring_at, 1 if incoming else 0)
        return pltpu.make_async_remote_copy(
            src_ref=gathered.at[h, at],
            dst_ref=gathered.at[h, at],
            send_sem=pair_send.at[h],
            recv_sem=pair_recv.at[h],
            device_id=to_pair(),
            device_id_type=pl.DeviceIdType.MESH,
        )

    def ring_step(h, q, step):
        for direction in range(2):
            if step > 1:
                ring_copy(h, q, direction, step - 1, incoming=True).wait_recv()
            if in_flow(q, direction, step):
                ring_copy(h, q, direction, step).start()

    for h in range(2):
        pair_copy(h).start()
        ring_step(h, 0, 1)

    loads[1].wait()
    edge[slots] = jnp.zeros((rows, rows), BF16)
    edge_t[slots] = jnp.zeros((rows, rows), BF16)
    table_copy.wait()

    def turn(t, carry):
        edge_t[t] = edge[t].T
        return carry

    def fill_dense(n, carry):
        for c in range(members):
            dense[n, :, c * rows : (c + 1) * rows] = edge[table[0, n * members + c]]
        return carry

    def fill_dense_t(c, carry):
        for n in range(SPAN):
            dense_t[c, :, n * rows : (n + 1) * rows] = edge_t[table[0, n * members + c]]
        return carry

    lax.fori_loop(0, SPAN, fill_dense, 0)
    for h in range(2):
        pair_copy(h, incoming=True).wait_recv()
        ring_step(h, 1, 1)
    for h in range(2):
        for q in range(2):
            ring_step(h, q, 2)
    lax.fori_loop(0, slots, turn, 0)
    for step in range(3, reach + 1):
        for h in range(2):
            for q in range(2):
                ring_step(h, q, step)

    def part_copy(h, offset):
        i = h * SPAN + offset + HALO
        return pltpu.make_async_remote_copy(
            src_ref=part_out.at[h, offset + HALO],
            dst_ref=part_in.at[h, offset + HALO],
            send_sem=part_send.at[i],
            recv_sem=part_recv.at[i],
            device_id=to_blk(offset),
            device_id_type=pl.DeviceIdType.MESH,
        )

    centre = []
    for h in range(2):
        for q in range(2):
            ring_copy(h, q, q, reach, incoming=True).wait_recv()
        columns = gathered[h].reshape(members * rows, half)
        for offset in sorted(offsets, key=lambda o: -abs(o)):
            part_out[h, offset + HALO] = matmul(dense[offset + HALO], columns).astype(BF16)
            part_copy(h, offset).start()
        centre.append(matmul(dense[HALO], columns))

    loads[2].wait()
    loads[3].wait()
    pre_base[...] = matmul(feat_bf, w_self[...]) + bias[...]
    lax.fori_loop(0, members, fill_dense_t, 0)
    for load in loads[4:]:
        load.wait()

    pre_act = pre_base[...]
    for h in range(2):
        total = centre[h]
        for offset in sorted(offsets, key=abs):
            part_copy(h, offset).wait_recv()
            total = total + part_in[h, offset + HALO].astype(F32)
        pre_act = pre_act + matmul(total.astype(BF16), w_agg[h * half : (h + 1) * half, :])
    sigmoid_z = jax.nn.sigmoid(pre_act)
    hidden = (pre_act * sigmoid_z).astype(BF16)
    mixed = matmul(hidden, w_out[...])
    centred = mixed - jnp.mean(mixed, axis=-1, keepdims=True)
    variance = jnp.mean(centred * centred, axis=-1, keepdims=True)
    inv_std = lax.rsqrt(variance + LN_EPS)
    normed = centred * inv_std

    g_norm = grad[...] * gain[...]
    g_mixed = inv_std * (
        g_norm
        - jnp.mean(g_norm, axis=-1, keepdims=True)
        - normed * jnp.mean(g_norm * normed, axis=-1, keepdims=True)
    )
    g_hidden = matmul_nt(g_mixed.astype(BF16), w_out[...])
    g_pre = (g_hidden * sigmoid_z * (1.0 + pre_act * (1.0 - sigmoid_z))).astype(BF16)

    def near_copy(h, offset):
        i = h * SPAN + offset + HALO
        return pltpu.make_async_remote_copy(
            src_ref=near.at[h, HALO],
            dst_ref=near.at[h, HALO - offset],
            send_sem=near_send.at[i],
            recv_sem=near_recv.at[i],
            device_id=to_blk(offset),
            device_id_type=pl.DeviceIdType.MESH,
        )

    for h in range(2):
        near[h, HALO] = matmul_nt(g_pre, w_agg[h * half : (h + 1) * half, :]).astype(BF16)
        for offset in sorted(offsets, key=lambda o: -abs(o)):
            near_copy(h, offset).start()

    updated[...] = feats[...] + gain[...] * normed
    stores = [pltpu.make_async_copy(updated, updated_hbm, out_sems.at[0])]
    stores[0].start()
    own_grad[...] = grad[...] + matmul_nt(g_pre, w_self[...])

    def red_copy(h, q, direction, step):
        i = ring_id(h, q, direction, step)
        return pltpu.make_async_remote_copy(
            src_ref=red_out.at[i],
            dst_ref=red_in.at[i],
            send_sem=red_send.at[i],
            recv_sem=red_recv.at[i],
            device_id=to_ring(direction),
            device_id_type=pl.DeviceIdType.MESH,
        )

    def red_flow(q, direction, step):
        return step > 1 or q == direction

    def message(h, ring_pos, q):
        return matmul(dense_t[member(ring_pos, q)], near[h].reshape(SPAN * rows, half))

    def red_step(h, step):
        distance = reach + 1 - step
        for q in (1, 0):
            for direction in range(2):
                if not red_flow(q, direction, step):
                    continue
                total = message(h, ring_at + (distance if direction == 0 else -distance), q)
                if step > 1 and red_flow(q, direction, step - 1):
                    red_copy(h, q, direction, step - 1).wait_recv()
                    total = total + red_in[ring_id(h, q, direction, step - 1)].astype(F32)
                red_out[ring_id(h, q, direction, step)] = total.astype(BF16)
                red_copy(h, q, direction, step).start()

    def swap_copy(h):
        return pltpu.make_async_remote_copy(
            src_ref=swap_out.at[h],
            dst_ref=swap_in.at[h],
            send_sem=swap_send.at[h],
            recv_sem=swap_recv.at[h],
            device_id=to_pair(),
            device_id_type=pl.DeviceIdType.MESH,
        )

    def red_total(h, q):
        total = message(h, ring_at, q)
        for direction in range(2):
            red_copy(h, q, direction, reach).wait_recv()
            total = total + red_in[ring_id(h, q, direction, reach)].astype(F32)
        return total

    def tile_gradient(t, carry):
        rel = jnp.clip(lax.rem(dest_ref[0, t] - blk + HALO + blocks, blocks), 0, SPAN - 1)
        col = jnp.clip(col_ref[0, t], 0, members - 1)
        value = matmul_nt(near[0, rel], gathered[0, col]) + matmul_nt(near[1, rel], gathered[1, col])
        tile_grads[t] = jnp.where(t < count_ref[0], value, 0.0).astype(BF16)
        return carry

    shares = reach
    share = slots // shares

    def tile_share(k):
        lax.fori_loop(k * share, (k + 1) * share, tile_gradient, 0)
        store = pltpu.make_async_copy(
            tile_grads.at[pl.ds(k * share, share)],
            tile_grads_hbm.at[0, pl.ds(k * share, share)],
            out_sems.at[2 + k],
        )
        store.start()
        stores.append(store)

    for h in range(2):
        for offset in sorted(offsets, key=abs):
            near_copy(h, offset).wait_recv()
        red_step(h, 1)
    for step in range(2, reach + 1):
        tile_share(step - 2)
        for h in range(2):
            red_step(h, step)
    tile_share(reach - 1)
    for h in range(2):
        swap_out[h] = red_total(h, 1).astype(BF16)
        swap_copy(h).start()
    own = [red_total(h, 0) for h in range(2)]
    for h in range(2):
        swap_copy(h).wait_recv()
        at = slice(h * half, (h + 1) * half)
        grad_x[:, at] = own_grad[:, at] + (own[h] + swap_in[h].astype(F32))
    stores.append(pltpu.make_async_copy(grad_x, grad_x_hbm, out_sems.at[1]))
    stores[-1].start()

    for h in range(2):
        pair_copy(h).wait_send()
        swap_copy(h).wait_send()
        for offset in offsets:
            part_copy(h, offset).wait_send()
            near_copy(h, offset).wait_send()
        for q in range(2):
            for direction in range(2):
                for step in range(1, reach + 1):
                    if in_flow(q, direction, step):
                        ring_copy(h, q, direction, step).wait_send()
                    if red_flow(q, direction, step):
                        red_copy(h, q, direction, step).wait_send()
    for store in stores:
        store.wait()


def body(
    node_feats,
    dest_block,
    col_tile,
    tile_count,
    edge_tiles,
    w_self,
    w_agg,
    in_bias,
    w_out,
    out_gain,
    grad_out,
):
    rows, feat = node_feats.shape
    half = feat // 2
    slots = dest_block.shape[1]
    members = lax.axis_size("grp")
    reach = members // 4
    flows = 8 * reach
    table_lanes = -(-SPAN * members // 128) * 128
    smem = pl.BlockSpec(memory_space=pltpu.SMEM)
    anywhere = pl.BlockSpec(memory_space=pl.ANY)
    dma = pltpu.SemaphoreType.DMA
    return pl.pallas_call(
        kernel,
        out_shape=(
            jax.ShapeDtypeStruct((rows, feat), F32),
            jax.ShapeDtypeStruct((rows, feat), F32),
            jax.ShapeDtypeStruct((1, slots, rows, rows), BF16),
        ),
        in_specs=[smem] * 3 + [anywhere] * 8,
        out_specs=[anywhere] * 3,
        scratch_shapes=[
            pltpu.VMEM((rows, feat), F32),
            pltpu.VMEM((slots + 1, rows, rows), BF16),
            pltpu.VMEM((feat, feat), BF16),
            pltpu.VMEM((feat, feat), BF16),
            pltpu.VMEM((1, feat), F32),
            pltpu.VMEM((feat, feat), BF16),
            pltpu.VMEM((1, feat), F32),
            pltpu.VMEM((rows, feat), F32),
            pltpu.VMEM((rows, feat), F32),
            pltpu.VMEM((rows, feat), F32),
            pltpu.VMEM((slots, rows, rows), BF16),
            pltpu.VMEM((1, table_lanes), jnp.int32),
            pltpu.SMEM((1, table_lanes), jnp.int32),
            pltpu.VMEM((slots + 1, rows, rows), BF16),
            pltpu.VMEM((SPAN, rows, members * rows), BF16),
            pltpu.VMEM((members, rows, SPAN * rows), BF16),
            pltpu.VMEM((2, members, rows, half), BF16),
            pltpu.VMEM((2, SPAN, rows, half), BF16),
            pltpu.VMEM((2, SPAN, rows, half), BF16),
            pltpu.VMEM((2, SPAN, rows, half), BF16),
            pltpu.VMEM((flows, rows, half), BF16),
            pltpu.VMEM((flows, rows, half), BF16),
            pltpu.VMEM((2, rows, half), BF16),
            pltpu.VMEM((2, rows, half), BF16),
            pltpu.VMEM((rows, feat), F32),
            pltpu.VMEM((rows, feat), F32),
            dma((8,)),
            dma((2 + reach,)),
            dma(()),
            dma((flows,)),
            dma((flows,)),
            dma((2,)),
            dma((2,)),
            dma((2 * SPAN,)),
            dma((2 * SPAN,)),
            dma((2 * SPAN,)),
            dma((2 * SPAN,)),
            dma((flows,)),
            dma((flows,)),
            dma((2,)),
            dma((2,)),
        ],
        compiler_params=pltpu.CompilerParams(
            collective_id=0, has_side_effects=True, vmem_limit_bytes=56 * 1024 * 1024
        ),
    )(
        dest_block,
        col_tile,
        tile_count,
        node_feats,
        edge_tiles,
        w_self,
        w_agg,
        in_bias[None],
        w_out,
        out_gain[None],
        grad_out,
    )


def solution(mesh):
    shards = ("blk", "grp")
    return jax.shard_map(
        body,
        mesh=mesh,
        in_specs=(
            P(shards, None),
            P(shards, None),
            P(shards, None),
            P(shards),
            P(shards, None, None, None),
            P(),
            P(),
            P(),
            P(),
            P(),
            P(shards, None),
        ),
        out_specs=(P(shards, None), P(shards, None), P(shards, None, None, None)),
        check_vma=False,
    )
```

```python
import jax
import jax.numpy as jnp
from jax import lax
from jax.experimental import pallas as pl
from jax.experimental.pallas import tpu as pltpu
from jax.sharding import PartitionSpec as P

HALO = 3
SPAN = 2 * HALO + 1
LN_EPS = 1e-05
BF16 = jnp.bfloat16
F32 = jnp.float32


def matmul(left, right):
    return jnp.dot(left, right, preferred_element_type=F32)


def matmul_nt(left, right):
    return lax.dot_general(left, right, (((1,), (1,)), ((), ())), preferred_element_type=F32)


def kernel(
    dest_hbm,
    col_hbm,
    count_hbm,
    feats_hbm,
    edge_hbm,
    w_self_hbm,
    w_agg_hbm,
    bias_hbm,
    w_out_hbm,
    gain_hbm,
    grad_hbm,
    updated_hbm,
    grad_x_hbm,
    tile_grads_hbm,
    dest,
    col,
    count,
    feats,
    edge,
    w_self,
    w_agg,
    bias,
    w_out,
    gain,
    grad,
    updated,
    grad_x,
    tile_grads,
    table_v,
    table,
    edge_t,
    dense,
    dense_t,
    gathered,
    part_out,
    part_in,
    near,
    red_out,
    red_in,
    swap_out,
    swap_in,
    messages,
    pre_base,
    own_grad,
    local_sems,
    out_sems,
    table_sem,
    ring_send,
    ring_recv,
    pair_send,
    pair_recv,
    part_send,
    part_recv,
    near_send,
    near_recv,
    red_send,
    red_recv,
    swap_send,
    swap_recv,
):
    rows = feats.shape[0]
    half = feats.shape[1] // 2
    slots = edge.shape[0] - 1
    members = gathered.shape[1]
    ring = members // 2
    reach = ring // 2
    blocks = lax.axis_size("blk")
    blk = lax.axis_index("blk")
    grp = lax.axis_index("grp")
    ring_at = grp // 2
    plane = grp % 2
    side = 2 * (blk % 2) - 1

    def member(ring_pos, q):
        return lax.rem(ring_pos + 2 * ring, ring) * 2 + (plane if q == 0 else 1 - plane)

    def to_ring(hop):
        return {"grp": member(ring_at + hop, 0)}

    def to_pair():
        return {"grp": member(ring_at, 1)}

    def to_blk(offset):
        return {"blk": lax.rem(blk + offset * side + blocks, blocks)}

    sent = []
    stores = []

    def send(copy):
        copy.start()
        sent.append(copy)

    def arrive(copy):
        copy.wait_recv()

    def finish():
        for copy in sent:
            copy.wait_send()
        for store in stores:
            store.wait()

    barrier = pltpu.get_barrier_semaphore()
    greeted = [to_pair()]
    greeted += [to_ring(hop) for hop in (-2, -1, 1, 2)]
    greeted += [to_blk(offset) for offset in (-1, 1, 2, -2, 3, -3)]
    for target in greeted:
        pl.semaphore_signal(barrier, inc=1, device_id=target, device_id_type=pl.DeviceIdType.MESH)

    loads = [
        pltpu.make_async_copy(src, dst, local_sems.at[i])
        for i, (src, dst) in enumerate(
            [
                (feats_hbm, feats),
                (dest_hbm, dest),
                (col_hbm, col),
                (count_hbm, count),
                (edge_hbm.at[0], edge.at[pl.ds(0, slots)]),
                (w_self_hbm, w_self),
                (bias_hbm, bias),
                (w_agg_hbm, w_agg),
                (w_out_hbm, w_out),
                (gain_hbm, gain),
                (grad_hbm, grad),
            ]
        )
    ]
    for load in loads:
        load.start()

    loads[0].wait()
    feat_bf = feats[...].astype(BF16)
    mine = member(ring_at, 0)
    for h in range(2):
        gathered[h, mine] = feat_bf[:, h * half : (h + 1) * half]

    pl.semaphore_wait(barrier, len(greeted))

    def ring_id(h, q, direction, d):
        return ((h * 2 + q) * 2 + direction) * reach + d - 1

    def in_flow(q, direction, d):
        return d < reach or direction == q and d == reach

    def ring_copy(h, q, direction, d, incoming=False):
        sign = 1 if direction == 0 else -1
        start = d - 1 if q == 0 else (0 if d <= 2 else 2)
        at = member(ring_at - sign * (d if incoming else start), q)
        i = ring_id(h, q, direction, d)
        return pltpu.make_async_remote_copy(
            src_ref=gathered.at[h, at],
            dst_ref=gathered.at[h, at],
            send_sem=ring_send.at[i],
            recv_sem=ring_recv.at[i],
            device_id=to_ring(sign * (d - start)),
            device_id_type=pl.DeviceIdType.MESH,
        )

    def pair_copy(h, incoming=False):
        at = member(ring_at, 1 if incoming else 0)
        return pltpu.make_async_remote_copy(
            src_ref=gathered.at[h, at],
            dst_ref=gathered.at[h, at],
            send_sem=pair_send.at[h],
            recv_sem=pair_recv.at[h],
            device_id=to_pair(),
            device_id_type=pl.DeviceIdType.MESH,
        )

    def ring_sends(h, q, *distances):
        for d in distances:
            for direction in range(2):
                if in_flow(q, direction, d):
                    send(ring_copy(h, q, direction, d))

    def ring_arrives(h, q, *distances):
        for d in distances:
            for direction in range(2):
                if in_flow(q, direction, d):
                    arrive(ring_copy(h, q, direction, d, incoming=True))

    def ring_arrives_last(h):
        ring_arrives(h, 1, 1, 3, 4)
        ring_arrives(h, 0, reach)

    for h in range(2):
        send(pair_copy(h))
        ring_sends(h, 0, 1)

    for load in loads[1:4]:
        load.wait()
    lane = lax.broadcasted_iota(jnp.int32, table_v.shape, 1)
    found = jnp.full(table_v.shape, slots, jnp.int32)
    for t in range(slots):
        rel = lax.rem(dest[0, t] - blk + HALO + blocks, blocks)
        key = jnp.where(t < count[0], rel * members + col[0, t], -1)
        found = jnp.where(lane == key, t, found)
    table_v[...] = found
    table_copy = pltpu.make_async_copy(table_v, table, table_sem)
    table_copy.start()

    loads[4].wait()
    edge[slots] = jnp.zeros((rows, rows), BF16)
    edge_t[slots] = jnp.zeros((rows, rows), BF16)

    def turn(t, carry):
        edge_t[t] = edge[t].T
        return carry

    def fill_dense(n, carry):
        for c in range(members):
            dense[n, :, c * rows : (c + 1) * rows] = edge[table[0, n * members + c]]
        return carry

    def fill_dense_t(q):
        def fill(k, carry):
            at = member(ring_at + k, q)
            for n in range(SPAN):
                dense_t[q, k, :, n * rows : (n + 1) * rows] = edge_t[table[0, n * members + at]]
            return carry

        lax.fori_loop(0, ring, fill, 0)

    for h in range(2):
        ring_arrives(h, 0, 1)
        ring_sends(h, 0, 2)
    table_copy.wait()
    lax.fori_loop(0, 3, fill_dense, 0)
    for h in range(2):
        ring_arrives(h, 0, 2)
        ring_sends(h, 0, 3)
    lax.fori_loop(3, SPAN, fill_dense, 0)
    for h in range(2):
        arrive(pair_copy(h, incoming=True))
        ring_sends(h, 1, 1, 2)
    for h in range(2):
        ring_arrives(h, 0, 3)
        ring_sends(h, 0, 4)
    lax.fori_loop(0, slots, turn, 0, unroll=2)
    for h in range(2):
        ring_arrives(h, 1, 2)
        ring_sends(h, 1, 3, 4)

    def part_copy(h, offset):
        i = h * SPAN + HALO + offset
        return pltpu.make_async_remote_copy(
            src_ref=part_out.at[h, HALO + offset],
            dst_ref=part_in.at[h, HALO + offset],
            send_sem=part_send.at[i],
            recv_sem=part_recv.at[i],
            device_id=to_blk(offset),
            device_id_type=pl.DeviceIdType.MESH,
        )

    centre = []
    for h in range(2):
        ring_arrives_last(h)
        columns = gathered[h].reshape(members * rows, half)
        for offset in (3, -3, 2, -2, 1, -1):
            partial = matmul(dense[HALO + offset * side], columns)
            part_out[h, HALO + offset] = partial.astype(BF16)
            send(part_copy(h, offset))
        centre.append(matmul(dense[HALO], columns))

    loads[5].wait()
    loads[6].wait()
    pre_base[...] = matmul(feat_bf, w_self[...]) + bias[...]
    for q in (1, 0):
        fill_dense_t(q)
    for load in loads[7:]:
        load.wait()

    pre_act = pre_base[...]
    for h in range(2):
        total = centre[h]
        for offset in (-1, 1, -2, 2, -3, 3):
            arrive(part_copy(h, offset))
            total = total + part_in[h, HALO + offset].astype(F32)
        pre_act = pre_act + matmul(total.astype(BF16), w_agg[h * half : (h + 1) * half, :])
    sigmoid_z = jax.nn.sigmoid(pre_act)
    hidden = (pre_act * sigmoid_z).astype(BF16)
    mixed = matmul(hidden, w_out[...])
    centred = mixed - jnp.mean(mixed, axis=-1, keepdims=True)
    variance = jnp.mean(centred * centred, axis=-1, keepdims=True)
    inv_std = lax.rsqrt(variance + LN_EPS)
    normed = centred * inv_std

    g_norm = grad[...] * gain[...]
    g_mixed = inv_std * (
        g_norm
        - jnp.mean(g_norm, axis=-1, keepdims=True)
        - normed * jnp.mean(g_norm * normed, axis=-1, keepdims=True)
    )
    g_hidden = matmul_nt(g_mixed.astype(BF16), w_out[...])
    g_pre = (g_hidden * sigmoid_z * (1.0 + pre_act * (1.0 - sigmoid_z))).astype(BF16)

    def near_copy(h, kind, incoming=False):
        source = 0 if kind < 4 else kind - 3
        target = {0: -1, 1: 1, 2: -2, 3: 3, 4: -1, 5: -1}[kind]
        lands = {0: -1, 1: 1, 2: 2, 3: 3, 4: -2, 5: -3}[kind] if incoming else source - target
        i = h * 6 + kind
        return pltpu.make_async_remote_copy(
            src_ref=near.at[h, HALO + source * side],
            dst_ref=near.at[h, HALO + lands * side],
            send_sem=near_send.at[i],
            recv_sem=near_recv.at[i],
            device_id=to_blk(target),
            device_id_type=pl.DeviceIdType.MESH,
        )

    for h in range(2):
        near[h, HALO] = matmul_nt(g_pre, w_agg[h * half : (h + 1) * half, :]).astype(BF16)
        for kind in (2, 1, 3, 0):
            send(near_copy(h, kind))

    updated[...] = feats[...] + gain[...] * normed
    stores.append(pltpu.make_async_copy(updated, updated_hbm, out_sems.at[0]))
    stores[-1].start()
    own_grad[...] = grad[...] + matmul_nt(g_pre, w_self[...])

    def red_flow(q, direction, d):
        return d < reach or direction == q and d == reach

    def red_hop(q, d):
        return 1 if q == 0 else (1 if d % 2 else 2)

    def red_copy(h, q, direction, d):
        i = ring_id(h, q, direction, d)
        return pltpu.make_async_remote_copy(
            src_ref=red_out.at[i],
            dst_ref=red_in.at[i],
            send_sem=red_send.at[i],
            recv_sem=red_recv.at[i],
            device_id=to_ring((1 if direction == 0 else -1) * red_hop(q, d)),
            device_id_type=pl.DeviceIdType.MESH,
        )

    def make_messages(h, q):
        made = matmul(
            dense_t[q].reshape(ring * rows, SPAN * rows), near[h].reshape(SPAN * rows, half)
        )
        messages[h, q] = made.reshape(ring, rows, half)

    def add_arrived(total, h, q, direction, distances):
        for d in distances:
            if red_flow(q, direction, d):
                arrive(red_copy(h, q, direction, d))
                total = total + red_in[ring_id(h, q, direction, d)].astype(F32)
        return total

    def red_sends(h, q, *distances):
        for d in distances:
            for direction in range(2):
                if red_flow(q, direction, d):
                    total = messages[h, q, (d if direction == 0 else -d) % ring]
                    earlier = [d + 1] if q == 0 else ([3, 4] if d == 2 else [])
                    total = add_arrived(total, h, q, direction, earlier)
                    red_out[ring_id(h, q, direction, d)] = total.astype(BF16)
                    send(red_copy(h, q, direction, d))

    def red_total(h, q):
        total = messages[h, q, 0]
        for direction in range(2):
            total = add_arrived(total, h, q, direction, [1, 2] if q else [1])
        return total

    def swap_copy(h):
        return pltpu.make_async_remote_copy(
            src_ref=swap_out.at[h],
            dst_ref=swap_in.at[h],
            send_sem=swap_send.at[h],
            recv_sem=swap_recv.at[h],
            device_id=to_pair(),
            device_id_type=pl.DeviceIdType.MESH,
        )

    def swap_sends(h):
        swap_out[h] = red_total(h, 1).astype(BF16)
        send(swap_copy(h))

    def tile_gradient(t, carry):
        rel = jnp.clip(lax.rem(dest[0, t] - blk + HALO + blocks, blocks), 0, SPAN - 1)
        at = jnp.clip(col[0, t], 0, members - 1)
        left = jnp.concatenate([near[0, rel], near[1, rel]], axis=1)
        right = jnp.concatenate([gathered[0, at], gathered[1, at]], axis=1)
        value = matmul_nt(left, right)
        tile_grads[t] = jnp.where(t < count[0], value, 0.0).astype(BF16)
        return carry

    share = slots // 4

    def tile_share(k):
        lax.fori_loop(k * share, (k + 1) * share, tile_gradient, 0, unroll=3 if share % 3 == 0 else 1)
        store = pltpu.make_async_copy(
            tile_grads.at[pl.ds(k * share, share)],
            tile_grads_hbm.at[0, pl.ds(k * share, share)],
            out_sems.at[2 + k],
        )
        store.start()
        stores.append(store)

    for h in range(2):
        for kind in (1, 2):
            arrive(near_copy(h, kind, incoming=True))
            send(near_copy(h, kind + 3))
        for kind in (0, 3, 4, 5):
            arrive(near_copy(h, kind, incoming=True))
        make_messages(h, 1)
        red_sends(h, 1, 4, 3)
        make_messages(h, 0)
        red_sends(h, 0, 4)
        red_sends(h, 1, 1)
    for h in range(2):
        red_sends(h, 1, 2)
        red_sends(h, 0, 3)
    tile_share(0)
    tile_share(1)
    for h in range(2):
        swap_sends(h)
    for h in range(2):
        red_sends(h, 0, 2)
    tile_share(2)
    for h in range(2):
        red_sends(h, 0, 1)
    tile_share(3)
    for h in range(2):
        total = red_total(h, 0)
        arrive(swap_copy(h))
        total = total + swap_in[h].astype(F32)
        at = slice(h * half, (h + 1) * half)
        grad_x[:, at] = own_grad[:, at] + total
    stores.append(pltpu.make_async_copy(grad_x, grad_x_hbm, out_sems.at[1]))
    stores[-1].start()

    finish()


def deliver(*refs):
    sources, targets, held = refs[:3], refs[3:6], refs[6:9]
    load_sems, store_sems = refs[9:]
    count = sources[2].shape[1] // 4
    pieces = [(2, (0, pl.ds(k * count, count))) for k in range(4)] + [(0, ...), (1, ...)]
    loads = [
        pltpu.make_async_copy(sources[a].at[at], held[a].at[at], load_sems.at[i])
        for i, (a, at) in enumerate(pieces)
    ]
    stores = [
        pltpu.make_async_copy(held[a].at[at], targets[a].at[at], store_sems.at[i])
        for i, (a, at) in enumerate(pieces)
    ]
    for load in loads:
        load.start()
    for load, store in zip(loads, stores):
        load.wait()
        store.start()
    for store in stores:
        store.wait()


def body(
    node_feats,
    dest_block,
    col_tile,
    tile_count,
    edge_tiles,
    w_self,
    w_agg,
    in_bias,
    w_out,
    out_gain,
    grad_out,
):
    rows, feat = node_feats.shape
    half = feat // 2
    slots = dest_block.shape[1]
    members = lax.axis_size("grp")
    reach = members // 4
    flows = 8 * reach
    table_lanes = -(-SPAN * members // 128) * 128
    anywhere = pl.BlockSpec(memory_space=pl.ANY)
    dma = pltpu.SemaphoreType.DMA
    results = (
        jax.ShapeDtypeStruct((rows, feat), F32),
        jax.ShapeDtypeStruct((rows, feat), F32),
        jax.ShapeDtypeStruct((1, slots, rows, rows), BF16),
    )
    made = pl.pallas_call(
        kernel,
        out_shape=results,
        in_specs=[anywhere] * 11,
        out_specs=[anywhere] * 3,
        scratch_shapes=[
            pltpu.SMEM((1, slots), jnp.int32),
            pltpu.SMEM((1, slots), jnp.int32),
            pltpu.SMEM((1,), jnp.int32),
            pltpu.VMEM((rows, feat), F32),
            pltpu.VMEM((slots + 1, rows, rows), BF16),
            pltpu.VMEM((feat, feat), BF16),
            pltpu.VMEM((feat, feat), BF16),
            pltpu.VMEM((1, feat), F32),
            pltpu.VMEM((feat, feat), BF16),
            pltpu.VMEM((1, feat), F32),
            pltpu.VMEM((rows, feat), F32),
            pltpu.VMEM((rows, feat), F32),
            pltpu.VMEM((rows, feat), F32),
            pltpu.VMEM((slots, rows, rows), BF16),
            pltpu.VMEM((1, table_lanes), jnp.int32),
            pltpu.SMEM((1, table_lanes), jnp.int32),
            pltpu.VMEM((slots + 1, rows, rows), BF16),
            pltpu.VMEM((SPAN, rows, members * rows), BF16),
            pltpu.VMEM((2, members // 2, rows, SPAN * rows), BF16),
            pltpu.VMEM((2, members, rows, half), BF16),
            pltpu.VMEM((2, SPAN, rows, half), BF16),
            pltpu.VMEM((2, SPAN, rows, half), BF16),
            pltpu.VMEM((2, SPAN, rows, half), BF16),
            pltpu.VMEM((flows, rows, half), BF16),
            pltpu.VMEM((flows, rows, half), BF16),
            pltpu.VMEM((4, rows, half), BF16),
            pltpu.VMEM((4, rows, half), BF16),
            pltpu.VMEM((2, 2, members // 2, rows, half), F32),
            pltpu.VMEM((rows, feat), F32),
            pltpu.VMEM((rows, feat), F32),
            dma((11,)),
            dma((6,)),
            dma(()),
            dma((flows,)),
            dma((flows,)),
            dma((4,)),
            dma((4,)),
            dma((2 * SPAN,)),
            dma((2 * SPAN,)),
            dma((12,)),
            dma((12,)),
            dma((flows,)),
            dma((flows,)),
            dma((4,)),
            dma((4,)),
        ],
        compiler_params=pltpu.CompilerParams(
            collective_id=0, has_side_effects=True, vmem_limit_bytes=56 * 1024 * 1024
        ),
    )(
        dest_block,
        col_tile,
        tile_count,
        node_feats,
        edge_tiles,
        w_self,
        w_agg,
        in_bias[None],
        w_out,
        out_gain[None],
        grad_out,
    )
    return pl.pallas_call(
        deliver,
        out_shape=results,
        in_specs=[anywhere] * 3,
        out_specs=[anywhere] * 3,
        scratch_shapes=[pltpu.VMEM(made_one.shape, made_one.dtype) for made_one in results]
        + [dma((6,)), dma((6,))],
        compiler_params=pltpu.CompilerParams(vmem_limit_bytes=56 * 1024 * 1024),
    )(*made)


def solution(mesh):
    shards = ("blk", "grp")
    return jax.shard_map(
        body,
        mesh=mesh,
        in_specs=(
            P(shards, None),
            P(shards, None),
            P(shards, None),
            P(shards),
            P(shards, None, None, None),
            P(),
            P(),
            P(),
            P(),
            P(),
            P(shards, None),
        ),
        out_specs=(P(shards, None), P(shards, None), P(shards, None, None, None)),
        check_vma=False,
    )
```

```python
import jax
import jax.numpy as jnp
from jax import lax
from jax.experimental import pallas as pl
from jax.experimental.pallas import tpu as pltpu
from jax.sharding import PartitionSpec as P

HALO = 3
SPAN = 2 * HALO + 1
LN_EPS = 1e-05
BF16 = jnp.bfloat16
F32 = jnp.float32


def matmul(left, right):
    return jnp.dot(left, right, preferred_element_type=F32)


def matmul_nt(left, right):
    return lax.dot_general(left, right, (((1,), (1,)), ((), ())), preferred_element_type=F32)


def kernel(
    dest_hbm,
    col_hbm,
    count_hbm,
    feats_hbm,
    edge_hbm,
    w_self_hbm,
    w_agg_hbm,
    bias_hbm,
    w_out_hbm,
    gain_hbm,
    grad_hbm,
    updated,
    grad_x,
    tile_grads,
    dest,
    col,
    count,
    feats,
    edge,
    w_self,
    w_agg,
    bias,
    w_out,
    gain,
    grad,
    table_v,
    table,
    edge_t,
    dense,
    dense_t,
    gathered,
    part_out,
    part_in,
    near,
    red_out,
    red_in,
    swap_out,
    swap_in,
    messages,
    w_agg_t,
    w_out_t,
    pre_base,
    own_grad,
    local_sems,
    table_sem,
    ring_send,
    ring_recv,
    pair_send,
    pair_recv,
    part_send,
    part_recv,
    near_send,
    near_recv,
    red_send,
    red_recv,
    swap_send,
    swap_recv,
):
    rows = feats.shape[0]
    half = feats.shape[1] // 2
    slots = edge.shape[0] - 1
    members = gathered.shape[1]
    ring = members // 2
    reach = ring // 2
    blocks = lax.axis_size("blk")
    blk = lax.axis_index("blk")
    grp = lax.axis_index("grp")
    ring_at = grp // 2
    plane = grp % 2
    side = 2 * (blk % 2) - 1

    def member(ring_pos, q):
        return lax.rem(ring_pos + 2 * ring, ring) * 2 + (plane if q == 0 else 1 - plane)

    def to_ring(hop):
        return {"grp": member(ring_at + hop, 0)}

    def to_pair():
        return {"grp": member(ring_at, 1)}

    def to_blk(offset):
        return {"blk": lax.rem(blk + offset * side + blocks, blocks)}

    sent = []

    def send(copy):
        copy.start()
        sent.append(copy)

    def arrive(copy):
        copy.wait_recv()

    def finish():
        for copy in sent:
            copy.wait_send()

    barrier = pltpu.get_barrier_semaphore()
    greeted = [to_pair()]
    greeted += [to_ring(hop) for hop in (-2, -1, 1, 2)]
    greeted += [to_blk(offset) for offset in (-1, 1, 2, -2, 3, -3)]
    for target in greeted:
        pl.semaphore_signal(barrier, inc=1, device_id=target, device_id_type=pl.DeviceIdType.MESH)

    loads = [
        pltpu.make_async_copy(src, dst, local_sems.at[i])
        for i, (src, dst) in enumerate(
            [
                (feats_hbm, feats),
                (dest_hbm, dest),
                (col_hbm, col),
                (count_hbm, count),
                (edge_hbm.at[0], edge.at[pl.ds(0, slots)]),
                (w_self_hbm, w_self),
                (bias_hbm, bias),
                (w_agg_hbm, w_agg),
                (w_out_hbm, w_out),
                (gain_hbm, gain),
                (grad_hbm, grad),
            ]
        )
    ]
    for load in loads:
        load.start()

    loads[0].wait()
    feat_bf = feats[...].astype(BF16)
    mine = member(ring_at, 0)
    for h in range(2):
        gathered[h, mine] = feat_bf[:, h * half : (h + 1) * half]

    pl.semaphore_wait(barrier, len(greeted))

    def ring_id(h, q, direction, d):
        return ((h * 2 + q) * 2 + direction) * reach + d - 1

    def in_flow(q, direction, d):
        return d < reach or direction == q and d == reach

    def ring_copy(h, q, direction, d, incoming=False):
        sign = 1 if direction == 0 else -1
        start = d - 1 if q == 0 else (0 if d <= 2 else 2)
        at = member(ring_at - sign * (d if incoming else start), q)
        i = ring_id(h, q, direction, d)
        return pltpu.make_async_remote_copy(
            src_ref=gathered.at[h, at],
            dst_ref=gathered.at[h, at],
            send_sem=ring_send.at[i],
            recv_sem=ring_recv.at[i],
            device_id=to_ring(sign * (d - start)),
            device_id_type=pl.DeviceIdType.MESH,
        )

    def pair_copy(h, incoming=False):
        at = member(ring_at, 1 if incoming else 0)
        return pltpu.make_async_remote_copy(
            src_ref=gathered.at[h, at],
            dst_ref=gathered.at[h, at],
            send_sem=pair_send.at[h],
            recv_sem=pair_recv.at[h],
            device_id=to_pair(),
            device_id_type=pl.DeviceIdType.MESH,
        )

    def ring_sends(h, q, *distances):
        for d in distances:
            for direction in range(2):
                if in_flow(q, direction, d):
                    send(ring_copy(h, q, direction, d))

    def ring_arrives(h, q, *distances):
        for d in distances:
            for direction in range(2):
                if in_flow(q, direction, d):
                    arrive(ring_copy(h, q, direction, d, incoming=True))

    def ring_arrives_last(h):
        ring_arrives(h, 1, 1, 3, 4)
        ring_arrives(h, 0, reach)

    for h in range(2):
        send(pair_copy(h))
        ring_sends(h, 0, 1)

    for load in loads[1:4]:
        load.wait()
    lane = lax.broadcasted_iota(jnp.int32, table_v.shape, 1)
    found = jnp.full(table_v.shape, slots, jnp.int32)
    for t in range(slots):
        rel = lax.rem(dest[0, t] - blk + HALO + blocks, blocks)
        key = jnp.where(t < count[0], rel * members + col[0, t], -1)
        found = jnp.where(lane == key, t, found)
    table_v[...] = found
    table_copy = pltpu.make_async_copy(table_v, table, table_sem)
    table_copy.start()

    loads[4].wait()
    edge[slots] = jnp.zeros((rows, rows), BF16)
    edge_t[slots] = jnp.zeros((rows, rows), BF16)

    def turn(t, carry):
        edge_t[t] = edge[t].T
        return carry

    def fill_dense(n, carry):
        for c in range(members):
            dense[n, :, c * rows : (c + 1) * rows] = edge[table[0, n * members + c]]
        return carry

    def fill_dense_t(q):
        def fill(k, carry):
            at = member(ring_at + k, q)
            for n in range(SPAN):
                dense_t[q, k, :, n * rows : (n + 1) * rows] = edge_t[table[0, n * members + at]]
            return carry

        lax.fori_loop(0, ring, fill, 0)

    for h in range(2):
        ring_arrives(h, 0, 1)
        ring_sends(h, 0, 2)
    table_copy.wait()
    lax.fori_loop(0, 3, fill_dense, 0)
    for h in range(2):
        ring_arrives(h, 0, 2)
        ring_sends(h, 0, 3)
    lax.fori_loop(3, SPAN, fill_dense, 0)
    for h in range(2):
        arrive(pair_copy(h, incoming=True))
        ring_sends(h, 1, 2)
    for h in range(2):
        ring_sends(h, 1, 1)
    for h in range(2):
        ring_arrives(h, 0, 3)
        ring_sends(h, 0, 4)
    lax.fori_loop(0, slots, turn, 0, unroll=2)
    for h in range(2):
        ring_arrives(h, 1, 2)
        ring_sends(h, 1, 4, 3)

    def part_copy(h, offset):
        i = h * SPAN + HALO + offset
        return pltpu.make_async_remote_copy(
            src_ref=part_out.at[h, HALO + offset],
            dst_ref=part_in.at[h, HALO + offset],
            send_sem=part_send.at[i],
            recv_sem=part_recv.at[i],
            device_id=to_blk(offset),
            device_id_type=pl.DeviceIdType.MESH,
        )

    centre = []
    for h in range(2):
        ring_arrives_last(h)
        columns = gathered[h].reshape(members * rows, half)
        for offset in (3, -3, 2, -2, 1, -1):
            partial = matmul(dense[HALO + offset * side], columns)
            part_out[h, HALO + offset] = partial.astype(BF16)
            send(part_copy(h, offset))
        centre.append(matmul(dense[HALO], columns))

    loads[5].wait()
    loads[6].wait()
    pre_base[...] = matmul(feat_bf, w_self[...]) + bias[...]
    for q in (1, 0):
        fill_dense_t(q)
    for load in loads[7:]:
        load.wait()
    w_agg_t[...] = w_agg[...].T
    w_out_t[...] = w_out[...].T

    pre_act = pre_base[...]
    for h in range(2):
        total = centre[h]
        for offset in (-1, 1, -2, 2, -3, 3):
            arrive(part_copy(h, offset))
            total = total + part_in[h, HALO + offset].astype(F32)
        pre_act = pre_act + matmul(total.astype(BF16), w_agg[h * half : (h + 1) * half, :])
    sigmoid_z = jax.nn.sigmoid(pre_act)
    hidden = (pre_act * sigmoid_z).astype(BF16)
    mixed = matmul(hidden, w_out[...])
    centred = mixed - jnp.mean(mixed, axis=-1, keepdims=True)
    variance = jnp.mean(centred * centred, axis=-1, keepdims=True)
    inv_std = lax.rsqrt(variance + LN_EPS)
    normed = centred * inv_std

    g_norm = grad[...] * gain[...]
    g_mixed = inv_std * (
        g_norm
        - jnp.mean(g_norm, axis=-1, keepdims=True)
        - normed * jnp.mean(g_norm * normed, axis=-1, keepdims=True)
    )
    g_hidden = matmul(g_mixed.astype(BF16), w_out_t[...])
    g_pre = (g_hidden * sigmoid_z * (1.0 + pre_act * (1.0 - sigmoid_z))).astype(BF16)

    def near_copy(h, kind, incoming=False):
        source = 0 if kind < 4 else kind - 3
        target = {0: -1, 1: 1, 2: -2, 3: 3, 4: -1, 5: -1}[kind]
        lands = {0: -1, 1: 1, 2: 2, 3: 3, 4: -2, 5: -3}[kind] if incoming else source - target
        i = h * 6 + kind
        return pltpu.make_async_remote_copy(
            src_ref=near.at[h, HALO + source * side],
            dst_ref=near.at[h, HALO + lands * side],
            send_sem=near_send.at[i],
            recv_sem=near_recv.at[i],
            device_id=to_blk(target),
            device_id_type=pl.DeviceIdType.MESH,
        )

    for h in range(2):
        near[h, HALO] = matmul(g_pre, w_agg_t[:, h * half : (h + 1) * half]).astype(BF16)
        for kind in (2, 1, 3, 0):
            send(near_copy(h, kind))

    updated[...] = feats[...] + gain[...] * normed
    own_grad[...] = grad[...] + matmul_nt(g_pre, w_self[...])

    def red_flow(q, direction, d):
        return d < reach or direction == q and d == reach

    def red_hop(q, d):
        return 1 if q == 0 else (1 if d % 2 else 2)

    def red_copy(h, q, direction, d):
        i = ring_id(h, q, direction, d)
        return pltpu.make_async_remote_copy(
            src_ref=red_out.at[i],
            dst_ref=red_in.at[i],
            send_sem=red_send.at[i],
            recv_sem=red_recv.at[i],
            device_id=to_ring((1 if direction == 0 else -1) * red_hop(q, d)),
            device_id_type=pl.DeviceIdType.MESH,
        )

    def make_messages(h, q):
        made = matmul(
            dense_t[q].reshape(ring * rows, SPAN * rows), near[h].reshape(SPAN * rows, half)
        )
        messages[h, q] = made.reshape(ring, rows, half)

    def add_arrived(total, h, q, direction, distances):
        for d in distances:
            if red_flow(q, direction, d):
                arrive(red_copy(h, q, direction, d))
                total = total + red_in[ring_id(h, q, direction, d)].astype(F32)
        return total

    def red_sends(h, q, *distances):
        for d in distances:
            for direction in range(2):
                if red_flow(q, direction, d):
                    total = messages[h, q, (d if direction == 0 else -d) % ring]
                    earlier = [d + 1] if q == 0 else ([3, 4] if d == 2 else [])
                    total = add_arrived(total, h, q, direction, earlier)
                    red_out[ring_id(h, q, direction, d)] = total.astype(BF16)
                    send(red_copy(h, q, direction, d))

    def red_total(h, q):
        total = messages[h, q, 0]
        for direction in range(2):
            total = add_arrived(total, h, q, direction, [1, 2] if q else [1])
        return total

    def swap_copy(h):
        return pltpu.make_async_remote_copy(
            src_ref=swap_out.at[h],
            dst_ref=swap_in.at[h],
            send_sem=swap_send.at[h],
            recv_sem=swap_recv.at[h],
            device_id=to_pair(),
            device_id_type=pl.DeviceIdType.MESH,
        )

    def swap_sends(h):
        swap_out[h] = red_total(h, 1).astype(BF16)
        send(swap_copy(h))

    def tile_gradient(t, carry):
        rel = jnp.clip(lax.rem(dest[0, t] - blk + HALO + blocks, blocks), 0, SPAN - 1)
        at = jnp.clip(col[0, t], 0, members - 1)
        left = jnp.concatenate([near[0, rel], near[1, rel]], axis=1)
        right = jnp.concatenate([gathered[0, at], gathered[1, at]], axis=1)
        value = matmul_nt(left, right)
        tile_grads[0, t] = jnp.where(t < count[0], value, 0.0).astype(BF16)
        return carry

    share = slots // 4

    def tile_share(k):
        lax.fori_loop(k * share, (k + 1) * share, tile_gradient, 0, unroll=3 if share % 3 == 0 else 1)

    for h in range(2):
        for kind in (1, 2):
            arrive(near_copy(h, kind, incoming=True))
            send(near_copy(h, kind + 3))
        for kind in (0, 3, 4, 5):
            arrive(near_copy(h, kind, incoming=True))
        make_messages(h, 1)
        red_sends(h, 1, 4, 3)
        make_messages(h, 0)
        red_sends(h, 0, 4)
        red_sends(h, 1, 1)
    for h in range(2):
        red_sends(h, 1, 2)
        red_sends(h, 0, 3)
    tile_share(0)
    for h in range(2):
        swap_sends(h)
        red_sends(h, 0, 2)
    tile_share(1)
    for h in range(2):
        red_sends(h, 0, 1)
    tile_share(2)
    tile_share(3)
    for h in range(2):
        total = red_total(h, 0)
        arrive(swap_copy(h))
        total = total + swap_in[h].astype(F32)
        at = slice(h * half, (h + 1) * half)
        grad_x[:, at] = own_grad[:, at] + total

    finish()


def deliver(*refs):
    sources, targets, sems = refs[:3], refs[3:6], refs[6]
    count = sources[2].shape[1] // 4
    pieces = [(2, (0, pl.ds(k * count, count))) for k in range(4)] + [(0, ...), (1, ...)]
    copies = [
        pltpu.make_async_copy(sources[a].at[at], targets[a].at[at], sems.at[i])
        for i, (a, at) in enumerate(pieces)
    ]
    for copy in copies:
        copy.start()
    for copy in copies:
        copy.wait()


def body(
    node_feats,
    dest_block,
    col_tile,
    tile_count,
    edge_tiles,
    w_self,
    w_agg,
    in_bias,
    w_out,
    out_gain,
    grad_out,
):
    rows, feat = node_feats.shape
    half = feat // 2
    slots = dest_block.shape[1]
    members = lax.axis_size("grp")
    reach = members // 4
    flows = 8 * reach
    table_lanes = -(-SPAN * members // 128) * 128
    anywhere = pl.BlockSpec(memory_space=pl.ANY)
    in_vmem = pl.BlockSpec(memory_space=pltpu.VMEM)
    dma = pltpu.SemaphoreType.DMA
    results = (
        jax.ShapeDtypeStruct((rows, feat), F32),
        jax.ShapeDtypeStruct((rows, feat), F32),
        jax.ShapeDtypeStruct((1, slots, rows, rows), BF16),
    )
    made = pl.pallas_call(
        kernel,
        out_shape=tuple(pltpu.VMEM(r.shape, r.dtype) for r in results),
        in_specs=[anywhere] * 11,
        out_specs=[in_vmem] * 3,
        scratch_shapes=[
            pltpu.SMEM((1, slots), jnp.int32),
            pltpu.SMEM((1, slots), jnp.int32),
            pltpu.SMEM((1,), jnp.int32),
            pltpu.VMEM((rows, feat), F32),
            pltpu.VMEM((slots + 1, rows, rows), BF16),
            pltpu.VMEM((feat, feat), BF16),
            pltpu.VMEM((feat, feat), BF16),
            pltpu.VMEM((1, feat), F32),
            pltpu.VMEM((feat, feat), BF16),
            pltpu.VMEM((1, feat), F32),
            pltpu.VMEM((rows, feat), F32),
            pltpu.VMEM((1, table_lanes), jnp.int32),
            pltpu.SMEM((1, table_lanes), jnp.int32),
            pltpu.VMEM((slots + 1, rows, rows), BF16),
            pltpu.VMEM((SPAN, rows, members * rows), BF16),
            pltpu.VMEM((2, members // 2, rows, SPAN * rows), BF16),
            pltpu.VMEM((2, members, rows, half), BF16),
            pltpu.VMEM((2, SPAN, rows, half), BF16),
            pltpu.VMEM((2, SPAN, rows, half), BF16),
            pltpu.VMEM((2, SPAN, rows, half), BF16),
            pltpu.VMEM((flows, rows, half), BF16),
            pltpu.VMEM((flows, rows, half), BF16),
            pltpu.VMEM((4, rows, half), BF16),
            pltpu.VMEM((4, rows, half), BF16),
            pltpu.VMEM((2, 2, members // 2, rows, half), F32),
            pltpu.VMEM((feat, feat), BF16),
            pltpu.VMEM((feat, feat), BF16),
            pltpu.VMEM((rows, feat), F32),
            pltpu.VMEM((rows, feat), F32),
            dma((11,)),
            dma(()),
            dma((flows,)),
            dma((flows,)),
            dma((4,)),
            dma((4,)),
            dma((2 * SPAN,)),
            dma((2 * SPAN,)),
            dma((12,)),
            dma((12,)),
            dma((flows,)),
            dma((flows,)),
            dma((4,)),
            dma((4,)),
        ],
        compiler_params=pltpu.CompilerParams(
            collective_id=0, has_side_effects=True, vmem_limit_bytes=56 * 1024 * 1024
        ),
    )(
        dest_block,
        col_tile,
        tile_count,
        node_feats,
        edge_tiles,
        w_self,
        w_agg,
        in_bias[None],
        w_out,
        out_gain[None],
        grad_out,
    )
    return pl.pallas_call(
        deliver,
        out_shape=results,
        in_specs=[in_vmem] * 3,
        out_specs=[anywhere] * 3,
        scratch_shapes=[dma((6,))],
        compiler_params=pltpu.CompilerParams(vmem_limit_bytes=56 * 1024 * 1024),
    )(*[pltpu.with_memory_space_constraint(one, pltpu.VMEM) for one in made])


def solution(mesh):
    shards = ("blk", "grp")
    return jax.shard_map(
        body,
        mesh=mesh,
        in_specs=(
            P(shards, None),
            P(shards, None),
            P(shards, None),
            P(shards),
            P(shards, None, None, None),
            P(),
            P(),
            P(),
            P(),
            P(),
            P(shards, None),
        ),
        out_specs=(P(shards, None), P(shards, None), P(shards, None, None, None)),
        check_vma=False,
    )
```

```python
import jax
import jax.numpy as jnp
from jax import lax
from jax.experimental import pallas as pl
from jax.experimental.pallas import tpu as pltpu
from jax.sharding import PartitionSpec as P

HALO = 3
SPAN = 2 * HALO + 1
LN_EPS = 1e-05
BF16 = jnp.bfloat16
F32 = jnp.float32


def matmul(left, right):
    return jnp.dot(left, right, preferred_element_type=F32)


def matmul_nt(left, right):
    return lax.dot_general(left, right, (((1,), (1,)), ((), ())), preferred_element_type=F32)


def kernel(
    dest_hbm,
    col_hbm,
    count_hbm,
    feats_hbm,
    edge_hbm,
    w_self_hbm,
    w_agg_hbm,
    bias_hbm,
    w_out_hbm,
    gain_hbm,
    grad_hbm,
    updated,
    grad_x,
    tile_grads,
    dest,
    col,
    count,
    feats,
    edge,
    w_self,
    w_agg,
    bias,
    w_out,
    gain,
    grad,
    table_v,
    table,
    edge_t,
    dense,
    dense_t,
    gathered,
    part_out,
    part_in,
    near,
    red_out,
    red_in,
    swap_out,
    swap_in,
    messages,
    w_agg_t,
    w_out_t,
    pre_base,
    own_grad,
    local_sems,
    table_sem,
    ring_send,
    ring_recv,
    pair_send,
    pair_recv,
    pair_here,
    part_send,
    part_recv,
    near_send,
    near_recv,
    red_send,
    red_recv,
    swap_send,
    swap_recv,
):
    rows = feats.shape[0]
    half = feats.shape[1] // 2
    slots = edge.shape[0] - 1
    members = gathered.shape[1]
    ring = members // 2
    reach = ring // 2
    blocks = lax.axis_size("blk")
    blk = lax.axis_index("blk")
    grp = lax.axis_index("grp")
    ring_at = grp // 2
    plane = grp % 2
    side = 2 * (blk % 2) - 1

    def member(ring_pos, q):
        return lax.rem(ring_pos + 2 * ring, ring) * 2 + (plane if q == 0 else 1 - plane)

    def to_ring(hop):
        return {"grp": member(ring_at + hop, 0)}

    def to_pair():
        return {"grp": member(ring_at, 1)}

    def to_blk(offset):
        return {"blk": lax.rem(blk + offset * side + blocks, blocks)}

    sent = []

    def send(copy, *which):
        copy(*which).start()
        sent.append((copy, which))

    def arrive(copy):
        copy.wait_recv()

    def finish():
        for copy, which in sent:
            copy(*which).wait_send()

    barrier = pltpu.get_barrier_semaphore()
    greeted = [to_ring(hop) for hop in (-2, -1, 1, 2)]
    greeted += [to_blk(offset) for offset in (-1, 1, 2, -2, 3, -3)]

    def greet(semaphore, target):
        pl.semaphore_signal(semaphore, inc=1, device_id=target, device_id_type=pl.DeviceIdType.MESH)

    @pl.when(plane == 0)
    def _():
        greet(barrier, to_pair())

    for target in greeted:
        greet(barrier, target)

    loads = [
        pltpu.make_async_copy(src, dst, local_sems.at[i])
        for i, (src, dst) in enumerate(
            [
                (feats_hbm, feats),
                (dest_hbm, dest),
                (col_hbm, col),
                (count_hbm, count),
                (edge_hbm.at[0], edge.at[pl.ds(0, slots)]),
                (w_self_hbm, w_self),
                (bias_hbm, bias),
                (w_agg_hbm, w_agg),
                (w_out_hbm, w_out),
                (gain_hbm, gain),
                (grad_hbm, grad),
            ]
        )
    ]
    for load in loads:
        load.start()

    loads[0].wait()
    feat_bf = feats[...].astype(BF16)
    mine = member(ring_at, 0)
    for h in range(2):
        gathered[h, mine] = feat_bf[:, h * half : (h + 1) * half]

    pl.semaphore_wait(barrier, len(greeted) + plane)

    @pl.when(plane == 1)
    def _():
        greet(pair_here, to_pair())

    def ring_id(h, q, direction, d):
        return ((h * 2 + min(q, 1)) * 2 + direction) * reach + d - 1

    def in_flow(h, q, direction, d):
        if q == 2:
            return d <= 3
        return d < reach or direction == (q + h) % 2 and d == reach

    def ring_copy(h, q, direction, d, incoming=False):
        sign = 1 if direction == 0 else -1
        if q == 2:
            hop = 1 if d == 3 else d
            start = reach if d == 3 else 0
            at = member(ring_at + start - (sign * hop if incoming else 0), 1)
        else:
            start = d - 1 if q == 0 else (0 if d <= 2 else 2)
            hop = d - start
            at = member(ring_at - sign * (d if incoming else start), q)
        i = ring_id(h, q, direction, d)
        return pltpu.make_async_remote_copy(
            src_ref=gathered.at[h, at],
            dst_ref=gathered.at[h, at],
            send_sem=ring_send.at[i],
            recv_sem=ring_recv.at[i],
            device_id=to_ring(sign * hop),
            device_id_type=pl.DeviceIdType.MESH,
        )

    def pair_copy(h, far=0, incoming=False):
        at = member(ring_at + far * reach, 1 if incoming else 0)
        return pltpu.make_async_remote_copy(
            src_ref=gathered.at[h, at],
            dst_ref=gathered.at[h, at],
            send_sem=pair_send.at[2 * far + h],
            recv_sem=pair_recv.at[2 * far + h],
            device_id=to_pair(),
            device_id_type=pl.DeviceIdType.MESH,
        )

    def ring_sends(h, q, *distances):
        for d in distances:
            for direction in range(2):
                if in_flow(h, q, direction, d):
                    if q == 0:
                        send(ring_copy, h, q, direction, d)
                    else:
                        ring_copy(h, q, direction, d).start()

    def ring_arrives(h, q, *distances):
        for d in distances:
            for direction in range(2):
                if in_flow(h, q, direction, d):
                    arrive(ring_copy(h, q, direction, d, incoming=True))

    def ring_arrives_last(h):
        @pl.when(plane == 0)
        def _():
            ring_arrives(h, 1, 1, 3, 4)

        @pl.when(plane == 1)
        def _():
            ring_arrives(h, 2, 1, 3, 2)
            ring_arrives(h, 0, 4)

    def ring_leaves():
        for q in (1, 2):

            @pl.when(plane == q - 1)
            def _(q=q):
                for h in range(2):
                    for direction in range(2):
                        for d in range(1, reach + 1):
                            if in_flow(h, q, direction, d):
                                ring_copy(h, q, direction, d).wait_send()
                    if q == 1:
                        pair_copy(h, 1).wait_send()

    @pl.when(plane == 1)
    def _():
        for h in range(2):
            pair_copy(h).start()

    for h in range(2):
        ring_sends(h, 0, 1)

    for load in loads[1:4]:
        load.wait()
    lane = lax.broadcasted_iota(jnp.int32, table_v.shape, 1)
    found = jnp.full(table_v.shape, slots, jnp.int32)
    for t in range(slots):
        rel = lax.rem(dest[0, t] - blk + HALO + blocks, blocks)
        key = jnp.where(t < count[0], rel * members + col[0, t], -1)
        found = jnp.where(lane == key, t, found)
    table_v[...] = found
    table_copy = pltpu.make_async_copy(table_v, table, table_sem)
    table_copy.start()

    loads[4].wait()
    edge[slots] = jnp.zeros((rows, rows), BF16)
    edge_t[slots] = jnp.zeros((rows, rows), BF16)

    def turn(t, carry):
        edge_t[t] = edge[t].T
        return carry

    def fill_dense(n, carry):
        for c in range(members):
            dense[n, :, c * rows : (c + 1) * rows] = edge[table[0, n * members + c]]
        return carry

    def fill_dense_t(q):
        def fill(k, carry):
            at = member(ring_at + k, q)
            for n in range(SPAN):
                dense_t[q, k, :, n * rows : (n + 1) * rows] = edge_t[table[0, n * members + at]]
            return carry

        lax.fori_loop(0, ring, fill, 0)

    for h in range(2):
        ring_arrives(h, 0, 1)
        ring_sends(h, 0, 2)
    table_copy.wait()
    lax.fori_loop(0, 3, fill_dense, 0)
    for h in range(2):
        ring_arrives(h, 0, 2)
        ring_sends(h, 0, 3)
    lax.fori_loop(3, SPAN, fill_dense, 0)
    for h in range(2):
        ring_arrives(h, 0, 3)
        ring_sends(h, 0, 4)

    @pl.when(plane == 0)
    def _():
        pl.semaphore_wait(pair_here, 1)
        for h in range(2):
            pair_copy(h).start()
            ring_arrives(h, 0, 4)
            pair_copy(h, 1).start()
        for h in range(2):
            arrive(pair_copy(h, incoming=True))
            ring_sends(h, 1, 2)
        for h in range(2):
            ring_sends(h, 1, 1)

    lax.fori_loop(0, slots, turn, 0, unroll=2)

    @pl.when(plane == 0)
    def _():
        for h in range(2):
            ring_arrives(h, 1, 2)
            ring_sends(h, 1, 4, 3)

    @pl.when(plane == 1)
    def _():
        for h in range(2):
            arrive(pair_copy(h, incoming=True))
            ring_sends(h, 2, 2, 1)
            arrive(pair_copy(h, 1, incoming=True))
            ring_sends(h, 2, 3)

    def part_copy(h, offset):
        i = h * SPAN + HALO + offset
        return pltpu.make_async_remote_copy(
            src_ref=part_out.at[h, HALO + offset],
            dst_ref=part_in.at[h, HALO + offset],
            send_sem=part_send.at[i],
            recv_sem=part_recv.at[i],
            device_id=to_blk(offset),
            device_id_type=pl.DeviceIdType.MESH,
        )

    centre = []
    for h in range(2):
        ring_arrives_last(h)
        columns = gathered[h].reshape(members * rows, half)
        for offset in (3, -3, 2, -2, 1, -1):
            partial = matmul(dense[HALO + offset * side], columns)
            part_out[h, HALO + offset] = partial.astype(BF16)
            send(part_copy, h, offset)
        centre.append(matmul(dense[HALO], columns))

    loads[5].wait()
    loads[6].wait()
    pre_base[...] = matmul(feat_bf, w_self[...]) + bias[...]
    for q in (1, 0):
        fill_dense_t(q)
    for load in loads[7:]:
        load.wait()
    w_agg_t[...] = w_agg[...].T
    w_out_t[...] = w_out[...].T

    pre_act = pre_base[...]
    for h in range(2):
        total = centre[h]
        for offset in (-1, 1, -2, 2, -3, 3):
            arrive(part_copy(h, offset))
            total = total + part_in[h, HALO + offset].astype(F32)
        pre_act = pre_act + matmul(total.astype(BF16), w_agg[h * half : (h + 1) * half, :])
    sigmoid_z = jax.nn.sigmoid(pre_act)
    hidden = (pre_act * sigmoid_z).astype(BF16)
    mixed = matmul(hidden, w_out[...])
    centred = mixed - jnp.mean(mixed, axis=-1, keepdims=True)
    variance = jnp.mean(centred * centred, axis=-1, keepdims=True)
    inv_std = lax.rsqrt(variance + LN_EPS)
    normed = centred * inv_std

    g_norm = grad[...] * gain[...]
    g_mixed = inv_std * (
        g_norm
        - jnp.mean(g_norm, axis=-1, keepdims=True)
        - normed * jnp.mean(g_norm * normed, axis=-1, keepdims=True)
    )
    g_hidden = matmul(g_mixed.astype(BF16), w_out_t[...])
    g_pre = (g_hidden * sigmoid_z * (1.0 + pre_act * (1.0 - sigmoid_z))).astype(BF16)

    def near_copy(h, kind, incoming=False):
        source = 0 if kind < 4 else kind - 3
        target = {0: -1, 1: 1, 2: -2, 3: 3, 4: -1, 5: -1}[kind]
        lands = {0: -1, 1: 1, 2: 2, 3: 3, 4: -2, 5: -3}[kind] if incoming else source - target
        i = h * 6 + kind
        return pltpu.make_async_remote_copy(
            src_ref=near.at[h, HALO + source * side],
            dst_ref=near.at[h, HALO + lands * side],
            send_sem=near_send.at[i],
            recv_sem=near_recv.at[i],
            device_id=to_blk(target),
            device_id_type=pl.DeviceIdType.MESH,
        )

    for h in range(2):
        near[h, HALO] = matmul(g_pre, w_agg_t[:, h * half : (h + 1) * half]).astype(BF16)
        for kind in (2, 1, 3, 0):
            send(near_copy, h, kind)

    updated[...] = feats[...] + gain[...] * normed
    own_grad[...] = grad[...] + matmul_nt(g_pre, w_self[...])

    def red_hop(q, d):
        return 1 if q == 0 else (1 if d % 2 else 2)

    def red_copy(h, q, direction, d):
        i = ring_id(h, q, direction, d)
        return pltpu.make_async_remote_copy(
            src_ref=red_out.at[i],
            dst_ref=red_in.at[i],
            send_sem=red_send.at[i],
            recv_sem=red_recv.at[i],
            device_id=to_ring((1 if direction == 0 else -1) * red_hop(q, d)),
            device_id_type=pl.DeviceIdType.MESH,
        )

    def make_messages(h, q):
        made = matmul(
            dense_t[q].reshape(ring * rows, SPAN * rows), near[h].reshape(SPAN * rows, half)
        )
        messages[h, q] = made.reshape(ring, rows, half)

    def add_arrived(total, h, q, direction, distances):
        for d in distances:
            if in_flow(h, q, direction, d):
                arrive(red_copy(h, q, direction, d))
                total = total + red_in[ring_id(h, q, direction, d)].astype(F32)
        return total

    def red_sends(h, q, *distances):
        for d in distances:
            for direction in range(2):
                if in_flow(h, q, direction, d):
                    total = messages[h, q, (d if direction == 0 else -d) % ring]
                    earlier = [d + 1] if q == 0 else ([3, 4] if d == 2 else [])
                    total = add_arrived(total, h, q, direction, earlier)
                    red_out[ring_id(h, q, direction, d)] = total.astype(BF16)
                    send(red_copy, h, q, direction, d)

    def red_total(h, q):
        total = messages[h, q, 0]
        for direction in range(2):
            total = add_arrived(total, h, q, direction, [1, 2] if q else [1])
        return total

    def swap_copy(h):
        return pltpu.make_async_remote_copy(
            src_ref=swap_out.at[h],
            dst_ref=swap_in.at[h],
            send_sem=swap_send.at[h],
            recv_sem=swap_recv.at[h],
            device_id=to_pair(),
            device_id_type=pl.DeviceIdType.MESH,
        )

    def swap_sends(h):
        swap_out[h] = red_total(h, 1).astype(BF16)
        send(swap_copy, h)

    def tile_gradient(t, carry):
        rel = jnp.clip(lax.rem(dest[0, t] - blk + HALO + blocks, blocks), 0, SPAN - 1)
        at = jnp.clip(col[0, t], 0, members - 1)
        left = jnp.concatenate([near[0, rel], near[1, rel]], axis=1)
        right = jnp.concatenate([gathered[0, at], gathered[1, at]], axis=1)
        value = matmul_nt(left, right)
        tile_grads[0, t] = jnp.where(t < count[0], value, 0.0).astype(BF16)
        return carry

    share = slots // 4

    def tile_share(k):
        lax.fori_loop(k * share, (k + 1) * share, tile_gradient, 0, unroll=3 if share % 3 == 0 else 1)

    def near_arrives(h):
        for kind in (1, 2):
            arrive(near_copy(h, kind, incoming=True))
            send(near_copy, h, kind + 3)
        for kind in (0, 3, 4, 5):
            arrive(near_copy(h, kind, incoming=True))

    first_sent = len(sent)

    @pl.when(plane == 1)
    def _():
        for h in range(2):
            near_arrives(h)
            make_messages(h, 1)
            red_sends(h, 1, 4, 3, 1)
        for h in range(2):
            red_sends(h, 1, 2)
        for h in range(2):
            make_messages(h, 0)
        for h in range(2):
            swap_sends(h)
        for h in range(2):
            red_sends(h, 0, 4)
        for step in (3, 2, 1):
            tile_share(3 - step)
            for h in range(2):
                red_sends(h, 0, step)

    del sent[first_sent:]

    @pl.when(plane == 0)
    def _():
        for h in range(2):
            near_arrives(h)
            make_messages(h, 1)
            red_sends(h, 1, 4, 3)
            make_messages(h, 0)
            red_sends(h, 0, 4)
            red_sends(h, 1, 1)
        for h in range(2):
            red_sends(h, 1, 2)
            red_sends(h, 0, 3)
        tile_share(0)
        for h in range(2):
            red_sends(h, 0, 2)
            swap_sends(h)
        tile_share(1)
        for h in range(2):
            red_sends(h, 0, 1)
        tile_share(2)

    tile_share(3)
    for h in range(2):
        total = red_total(h, 0)
        arrive(swap_copy(h))
        total = total + swap_in[h].astype(F32)
        at = slice(h * half, (h + 1) * half)
        grad_x[:, at] = own_grad[:, at] + total

    for h in range(2):
        pair_copy(h).wait_send()
    ring_leaves()
    finish()


def deliver(*refs):
    sources, targets, sems = refs[:3], refs[3:6], refs[6]
    count = sources[2].shape[1] // 4
    pieces = [(2, (0, pl.ds(k * count, count))) for k in range(4)] + [(0, ...), (1, ...)]
    copies = [
        pltpu.make_async_copy(sources[a].at[at], targets[a].at[at], sems.at[i])
        for i, (a, at) in enumerate(pieces)
    ]
    for copy in copies:
        copy.start()
    for copy in copies:
        copy.wait()


def body(
    node_feats,
    dest_block,
    col_tile,
    tile_count,
    edge_tiles,
    w_self,
    w_agg,
    in_bias,
    w_out,
    out_gain,
    grad_out,
):
    rows, feat = node_feats.shape
    half = feat // 2
    slots = dest_block.shape[1]
    members = lax.axis_size("grp")
    reach = members // 4
    flows = 8 * reach
    table_lanes = -(-SPAN * members // 128) * 128
    anywhere = pl.BlockSpec(memory_space=pl.ANY)
    in_vmem = pl.BlockSpec(memory_space=pltpu.VMEM)
    dma = pltpu.SemaphoreType.DMA
    results = (
        jax.ShapeDtypeStruct((rows, feat), F32),
        jax.ShapeDtypeStruct((rows, feat), F32),
        jax.ShapeDtypeStruct((1, slots, rows, rows), BF16),
    )
    made = pl.pallas_call(
        kernel,
        out_shape=tuple(pltpu.VMEM(r.shape, r.dtype) for r in results),
        in_specs=[anywhere] * 11,
        out_specs=[in_vmem] * 3,
        scratch_shapes=[
            pltpu.SMEM((1, slots), jnp.int32),
            pltpu.SMEM((1, slots), jnp.int32),
            pltpu.SMEM((1,), jnp.int32),
            pltpu.VMEM((rows, feat), F32),
            pltpu.VMEM((slots + 1, rows, rows), BF16),
            pltpu.VMEM((feat, feat), BF16),
            pltpu.VMEM((feat, feat), BF16),
            pltpu.VMEM((1, feat), F32),
            pltpu.VMEM((feat, feat), BF16),
            pltpu.VMEM((1, feat), F32),
            pltpu.VMEM((rows, feat), F32),
            pltpu.VMEM((1, table_lanes), jnp.int32),
            pltpu.SMEM((1, table_lanes), jnp.int32),
            pltpu.VMEM((slots + 1, rows, rows), BF16),
            pltpu.VMEM((SPAN, rows, members * rows), BF16),
            pltpu.VMEM((2, members // 2, rows, SPAN * rows), BF16),
            pltpu.VMEM((2, members, rows, half), BF16),
            pltpu.VMEM((2, SPAN, rows, half), BF16),
            pltpu.VMEM((2, SPAN, rows, half), BF16),
            pltpu.VMEM((2, SPAN, rows, half), BF16),
            pltpu.VMEM((flows, rows, half), BF16),
            pltpu.VMEM((flows, rows, half), BF16),
            pltpu.VMEM((4, rows, half), BF16),
            pltpu.VMEM((4, rows, half), BF16),
            pltpu.VMEM((2, 2, members // 2, rows, half), F32),
            pltpu.VMEM((feat, feat), BF16),
            pltpu.VMEM((feat, feat), BF16),
            pltpu.VMEM((rows, feat), F32),
            pltpu.VMEM((rows, feat), F32),
            dma((11,)),
            dma(()),
            dma((flows,)),
            dma((flows,)),
            dma((4,)),
            dma((4,)),
            pltpu.SemaphoreType.REGULAR,
            dma((2 * SPAN,)),
            dma((2 * SPAN,)),
            dma((12,)),
            dma((12,)),
            dma((flows,)),
            dma((flows,)),
            dma((4,)),
            dma((4,)),
        ],
        compiler_params=pltpu.CompilerParams(
            collective_id=0, has_side_effects=True, vmem_limit_bytes=56 * 1024 * 1024
        ),
    )(
        dest_block,
        col_tile,
        tile_count,
        node_feats,
        edge_tiles,
        w_self,
        w_agg,
        in_bias[None],
        w_out,
        out_gain[None],
        grad_out,
    )
    return pl.pallas_call(
        deliver,
        out_shape=results,
        in_specs=[in_vmem] * 3,
        out_specs=[anywhere] * 3,
        scratch_shapes=[dma((6,))],
        compiler_params=pltpu.CompilerParams(vmem_limit_bytes=56 * 1024 * 1024),
    )(*[pltpu.with_memory_space_constraint(one, pltpu.VMEM) for one in made])


def solution(mesh):
    shards = ("blk", "grp")
    return jax.shard_map(
        body,
        mesh=mesh,
        in_specs=(
            P(shards, None),
            P(shards, None),
            P(shards, None),
            P(shards),
            P(shards, None, None, None),
            P(),
            P(),
            P(),
            P(),
            P(),
            P(shards, None),
        ),
        out_specs=(P(shards, None), P(shards, None), P(shards, None, None, None)),
        check_vma=False,
    )
```

```python
import jax
import jax.numpy as jnp
from jax import lax
from jax.experimental import pallas as pl
from jax.experimental.pallas import tpu as pltpu
from jax.sharding import PartitionSpec as P

HALO = 3
SPAN = 2 * HALO + 1
LN_EPS = 1e-05
BF16 = jnp.bfloat16
F32 = jnp.float32


def matmul(left, right):
    return jnp.dot(left, right, preferred_element_type=F32)


def matmul_nt(left, right):
    return lax.dot_general(left, right, (((1,), (1,)), ((), ())), preferred_element_type=F32)


def kernel(
    dest_hbm,
    col_hbm,
    count_hbm,
    feats_hbm,
    edge_hbm,
    w_self_hbm,
    w_agg_hbm,
    bias_hbm,
    w_out_hbm,
    gain_hbm,
    grad_hbm,
    updated,
    grad_x,
    tile_grads,
    dest,
    col,
    count,
    feats,
    edge,
    w_self,
    w_agg,
    bias,
    w_out,
    gain,
    grad,
    table_v,
    table,
    edge_t,
    dense,
    dense_t,
    gathered,
    part_out,
    part_in,
    near,
    red_out,
    red_in,
    swap_out,
    swap_in,
    messages,
    w_agg_t,
    w_out_t,
    pre_base,
    own_grad,
    local_sems,
    table_sem,
    ring_send,
    ring_recv,
    pair_send,
    pair_recv,
    part_send,
    part_recv,
    near_send,
    near_recv,
    red_send,
    red_recv,
    swap_send,
    swap_recv,
):
    rows = feats.shape[0]
    half = feats.shape[1] // 2
    slots = edge.shape[0] - 1
    members = gathered.shape[1]
    ring = members // 2
    reach = ring // 2
    blocks = lax.axis_size("blk")
    blk = lax.axis_index("blk")
    grp = lax.axis_index("grp")
    ring_at = grp // 2
    plane = grp % 2
    side = 2 * (blk % 2) - 1

    def member(ring_pos, q):
        return lax.rem(ring_pos + 2 * ring, ring) * 2 + (plane if q == 0 else 1 - plane)

    def to_ring(hop):
        return {"grp": member(ring_at + hop, 0)}

    def to_pair():
        return {"grp": member(ring_at, 1)}

    def to_blk(offset):
        return {"blk": lax.rem(blk + offset * side + blocks, blocks)}

    sent = []

    def send(copy):
        copy.start()
        sent.append(copy)

    def arrive(copy):
        copy.wait_recv()

    def finish():
        for copy in sent:
            copy.wait_send()

    barrier = pltpu.get_barrier_semaphore()
    greeted = [to_pair()]
    greeted += [to_ring(hop) for hop in (-2, -1, 1, 2)]
    greeted += [to_blk(offset) for offset in (-1, 1, 2, -2, 3, -3)]
    for target in greeted:
        pl.semaphore_signal(barrier, inc=1, device_id=target, device_id_type=pl.DeviceIdType.MESH)

    loads = [
        pltpu.make_async_copy(src, dst, local_sems.at[i])
        for i, (src, dst) in enumerate(
            [
                (feats_hbm, feats),
                (dest_hbm, dest),
                (col_hbm, col),
                (count_hbm, count),
                (edge_hbm.at[0], edge.at[pl.ds(0, slots)]),
                (w_self_hbm, w_self),
                (bias_hbm, bias),
                (w_agg_hbm, w_agg),
                (w_out_hbm, w_out),
                (gain_hbm, gain),
                (grad_hbm, grad),
            ]
        )
    ]
    for load in loads:
        load.start()

    loads[0].wait()
    feat_bf = feats[...].astype(BF16)
    mine = member(ring_at, 0)
    for h in range(2):
        gathered[h, mine] = feat_bf[:, h * half : (h + 1) * half]

    pl.semaphore_wait(barrier, len(greeted))

    def ring_id(h, q, direction, d):
        return ((h * 2 + q) * 2 + direction) * reach + d - 1

    def in_flow(h, q, direction, d):
        return d < reach or direction == (q + h) % 2 and d == reach

    def ring_copy(h, q, direction, d, incoming=False):
        sign = 1 if direction == 0 else -1
        start = d - 1 if q == 0 else (0 if d <= 2 else 2)
        at = member(ring_at - sign * (d if incoming else start), q)
        i = ring_id(h, q, direction, d)
        return pltpu.make_async_remote_copy(
            src_ref=gathered.at[h, at],
            dst_ref=gathered.at[h, at],
            send_sem=ring_send.at[i],
            recv_sem=ring_recv.at[i],
            device_id=to_ring(sign * (d - start)),
            device_id_type=pl.DeviceIdType.MESH,
        )

    def pair_copy(h, incoming=False):
        at = member(ring_at, 1 if incoming else 0)
        return pltpu.make_async_remote_copy(
            src_ref=gathered.at[h, at],
            dst_ref=gathered.at[h, at],
            send_sem=pair_send.at[h],
            recv_sem=pair_recv.at[h],
            device_id=to_pair(),
            device_id_type=pl.DeviceIdType.MESH,
        )

    def ring_sends(h, q, *distances):
        for d in distances:
            for direction in range(2):
                if in_flow(h, q, direction, d):
                    send(ring_copy(h, q, direction, d))

    def ring_arrives(h, q, *distances):
        for d in distances:
            for direction in range(2):
                if in_flow(h, q, direction, d):
                    arrive(ring_copy(h, q, direction, d, incoming=True))

    def ring_arrives_last(h):
        ring_arrives(h, 1, 1, 3, 4)
        ring_arrives(h, 0, reach)

    for h in range(2):
        send(pair_copy(h))
        ring_sends(h, 0, 1)

    for load in loads[1:4]:
        load.wait()
    lane = lax.broadcasted_iota(jnp.int32, table_v.shape, 1)
    found = jnp.full(table_v.shape, slots, jnp.int32)
    for t in range(slots):
        rel = lax.rem(dest[0, t] - blk + HALO + blocks, blocks)
        key = jnp.where(t < count[0], rel * members + col[0, t], -1)
        found = jnp.where(lane == key, t, found)
    table_v[...] = found
    table_copy = pltpu.make_async_copy(table_v, table, table_sem)
    table_copy.start()

    loads[4].wait()
    edge[slots] = jnp.zeros((rows, rows), BF16)
    edge_t[slots] = jnp.zeros((rows, rows), BF16)

    def turn(t, carry):
        edge_t[t] = edge[t].T
        return carry

    def fill_dense(n, carry):
        for c in range(members):
            dense[n, :, c * rows : (c + 1) * rows] = edge[table[0, n * members + c]]
        return carry

    def fill_dense_t(q):
        def fill(k, carry):
            at = member(ring_at + k, q)
            for n in range(SPAN):
                dense_t[q, k, :, n * rows : (n + 1) * rows] = edge_t[table[0, n * members + at]]
            return carry

        lax.fori_loop(0, ring, fill, 0)

    for h in range(2):
        ring_arrives(h, 0, 1)
        ring_sends(h, 0, 2)
    table_copy.wait()
    lax.fori_loop(0, 3, fill_dense, 0)
    for h in range(2):
        ring_arrives(h, 0, 2)
        ring_sends(h, 0, 3)
    lax.fori_loop(3, SPAN, fill_dense, 0)
    for h in range(2):
        arrive(pair_copy(h, incoming=True))
        ring_sends(h, 1, 2)
    for h in range(2):
        ring_sends(h, 1, 1)
    for h in range(2):
        ring_arrives(h, 0, 3)
        ring_sends(h, 0, 4)
    lax.fori_loop(0, slots, turn, 0, unroll=2)
    for h in range(2):
        ring_arrives(h, 1, 2)
        ring_sends(h, 1, 4, 3)

    def part_copy(h, offset):
        i = h * SPAN + HALO + offset
        return pltpu.make_async_remote_copy(
            src_ref=part_out.at[h, HALO + offset],
            dst_ref=part_in.at[h, HALO + offset],
            send_sem=part_send.at[i],
            recv_sem=part_recv.at[i],
            device_id=to_blk(offset),
            device_id_type=pl.DeviceIdType.MESH,
        )

    centre = []
    for h in range(2):
        ring_arrives_last(h)
        columns = gathered[h].reshape(members * rows, half)
        for offset in (3, -3, 2, -2, 1, -1):
            partial = matmul(dense[HALO + offset * side], columns)
            part_out[h, HALO + offset] = partial.astype(BF16)
            send(part_copy(h, offset))
        centre.append(matmul(dense[HALO], columns))

    loads[5].wait()
    loads[6].wait()
    pre_base[...] = matmul(feat_bf, w_self[...]) + bias[...]
    for q in (1, 0):
        fill_dense_t(q)
    for load in loads[7:]:
        load.wait()
    w_agg_t[...] = w_agg[...].T
    w_out_t[...] = w_out[...].T

    pre_act = pre_base[...]
    for h in range(2):
        total = centre[h]
        for offset in (-1, 1, -2, 2, -3, 3):
            arrive(part_copy(h, offset))
            total = total + part_in[h, HALO + offset].astype(F32)
        pre_act = pre_act + matmul(total.astype(BF16), w_agg[h * half : (h + 1) * half, :])
    sigmoid_z = jax.nn.sigmoid(pre_act)
    hidden = (pre_act * sigmoid_z).astype(BF16)
    mixed = matmul(hidden, w_out[...])
    centred = mixed - jnp.mean(mixed, axis=-1, keepdims=True)
    variance = jnp.mean(centred * centred, axis=-1, keepdims=True)
    inv_std = lax.rsqrt(variance + LN_EPS)
    normed = centred * inv_std

    g_norm = grad[...] * gain[...]
    g_mixed = inv_std * (
        g_norm
        - jnp.mean(g_norm, axis=-1, keepdims=True)
        - normed * jnp.mean(g_norm * normed, axis=-1, keepdims=True)
    )
    g_hidden = matmul(g_mixed.astype(BF16), w_out_t[...])
    g_pre = (g_hidden * sigmoid_z * (1.0 + pre_act * (1.0 - sigmoid_z))).astype(BF16)

    def near_copy(h, kind, incoming=False):
        source = 0 if kind < 4 else kind - 3
        target = {0: -1, 1: 1, 2: -2, 3: 3, 4: -1, 5: -1}[kind]
        lands = {0: -1, 1: 1, 2: 2, 3: 3, 4: -2, 5: -3}[kind] if incoming else source - target
        i = h * 6 + kind
        return pltpu.make_async_remote_copy(
            src_ref=near.at[h, HALO + source * side],
            dst_ref=near.at[h, HALO + lands * side],
            send_sem=near_send.at[i],
            recv_sem=near_recv.at[i],
            device_id=to_blk(target),
            device_id_type=pl.DeviceIdType.MESH,
        )

    for h in range(2):
        near[h, HALO] = matmul(g_pre, w_agg_t[:, h * half : (h + 1) * half]).astype(BF16)
        for kind in (2, 1, 3, 0):
            send(near_copy(h, kind))

    updated[...] = feats[...] + gain[...] * normed
    own_grad[...] = grad[...] + matmul_nt(g_pre, w_self[...])

    def red_hop(q, d):
        return 1 if q == 0 else (1 if d % 2 else 2)

    def red_copy(h, q, direction, d):
        i = ring_id(h, q, direction, d)
        return pltpu.make_async_remote_copy(
            src_ref=red_out.at[i],
            dst_ref=red_in.at[i],
            send_sem=red_send.at[i],
            recv_sem=red_recv.at[i],
            device_id=to_ring((1 if direction == 0 else -1) * red_hop(q, d)),
            device_id_type=pl.DeviceIdType.MESH,
        )

    def make_messages(h, q):
        made = matmul(
            dense_t[q].reshape(ring * rows, SPAN * rows), near[h].reshape(SPAN * rows, half)
        )
        messages[h, q] = made.reshape(ring, rows, half)

    def add_arrived(total, h, q, direction, distances):
        for d in distances:
            if in_flow(h, q, direction, d):
                arrive(red_copy(h, q, direction, d))
                total = total + red_in[ring_id(h, q, direction, d)].astype(F32)
        return total

    def red_sends(h, q, *distances):
        for d in distances:
            for direction in range(2):
                if in_flow(h, q, direction, d):
                    total = messages[h, q, (d if direction == 0 else -d) % ring]
                    earlier = [d + 1] if q == 0 else ([3, 4] if d == 2 else [])
                    total = add_arrived(total, h, q, direction, earlier)
                    red_out[ring_id(h, q, direction, d)] = total.astype(BF16)
                    send(red_copy(h, q, direction, d))

    def red_total(h, q):
        total = messages[h, q, 0]
        for direction in range(2):
            total = add_arrived(total, h, q, direction, [1, 2] if q else [1])
        return total

    def swap_copy(h):
        return pltpu.make_async_remote_copy(
            src_ref=swap_out.at[h],
            dst_ref=swap_in.at[h],
            send_sem=swap_send.at[h],
            recv_sem=swap_recv.at[h],
            device_id=to_pair(),
            device_id_type=pl.DeviceIdType.MESH,
        )

    def swap_sends(h):
        swap_out[h] = red_total(h, 1).astype(BF16)
        send(swap_copy(h))

    def tile_gradient(t, carry):
        rel = jnp.clip(lax.rem(dest[0, t] - blk + HALO + blocks, blocks), 0, SPAN - 1)
        at = jnp.clip(col[0, t], 0, members - 1)
        left = jnp.concatenate([near[0, rel], near[1, rel]], axis=1)
        right = jnp.concatenate([gathered[0, at], gathered[1, at]], axis=1)
        value = matmul_nt(left, right)
        tile_grads[0, t] = jnp.where(t < count[0], value, 0.0).astype(BF16)
        return carry

    share = slots // 4

    def tile_share(k):
        lax.fori_loop(k * share, (k + 1) * share, tile_gradient, 0, unroll=3 if share % 3 == 0 else 1)

    for h in range(2):
        for kind in (1, 2):
            arrive(near_copy(h, kind, incoming=True))
            send(near_copy(h, kind + 3))
        for kind in (0, 3, 4, 5):
            arrive(near_copy(h, kind, incoming=True))
        make_messages(h, 1)
        red_sends(h, 1, 4, 3)
        make_messages(h, 0)
        red_sends(h, 0, 4)
        red_sends(h, 1, 1)
    for h in range(2):
        red_sends(h, 1, 2)
        red_sends(h, 0, 3)
    tile_share(0)
    for h in range(2):
        red_sends(h, 0, 2)
        swap_sends(h)
    tile_share(1)
    for h in range(2):
        red_sends(h, 0, 1)
    tile_share(2)
    tile_share(3)
    for h in range(2):
        total = red_total(h, 0)
        arrive(swap_copy(h))
        total = total + swap_in[h].astype(F32)
        at = slice(h * half, (h + 1) * half)
        grad_x[:, at] = own_grad[:, at] + total

    finish()


def deliver(*refs):
    sources, targets, sems = refs[:3], refs[3:6], refs[6]
    count = sources[2].shape[1] // 4
    pieces = [(2, (0, pl.ds(k * count, count))) for k in range(4)] + [(0, ...), (1, ...)]
    copies = [
        pltpu.make_async_copy(sources[a].at[at], targets[a].at[at], sems.at[i])
        for i, (a, at) in enumerate(pieces)
    ]
    for copy in copies:
        copy.start()
    for copy in copies:
        copy.wait()


def body(
    node_feats,
    dest_block,
    col_tile,
    tile_count,
    edge_tiles,
    w_self,
    w_agg,
    in_bias,
    w_out,
    out_gain,
    grad_out,
):
    rows, feat = node_feats.shape
    half = feat // 2
    slots = dest_block.shape[1]
    members = lax.axis_size("grp")
    reach = members // 4
    flows = 8 * reach
    table_lanes = -(-SPAN * members // 128) * 128
    anywhere = pl.BlockSpec(memory_space=pl.ANY)
    in_vmem = pl.BlockSpec(memory_space=pltpu.VMEM)
    dma = pltpu.SemaphoreType.DMA
    results = (
        jax.ShapeDtypeStruct((rows, feat), F32),
        jax.ShapeDtypeStruct((rows, feat), F32),
        jax.ShapeDtypeStruct((1, slots, rows, rows), BF16),
    )
    made = pl.pallas_call(
        kernel,
        out_shape=tuple(pltpu.VMEM(r.shape, r.dtype) for r in results),
        in_specs=[anywhere] * 11,
        out_specs=[in_vmem] * 3,
        scratch_shapes=[
            pltpu.SMEM((1, slots), jnp.int32),
            pltpu.SMEM((1, slots), jnp.int32),
            pltpu.SMEM((1,), jnp.int32),
            pltpu.VMEM((rows, feat), F32),
            pltpu.VMEM((slots + 1, rows, rows), BF16),
            pltpu.VMEM((feat, feat), BF16),
            pltpu.VMEM((feat, feat), BF16),
            pltpu.VMEM((1, feat), F32),
            pltpu.VMEM((feat, feat), BF16),
            pltpu.VMEM((1, feat), F32),
            pltpu.VMEM((rows, feat), F32),
            pltpu.VMEM((1, table_lanes), jnp.int32),
            pltpu.SMEM((1, table_lanes), jnp.int32),
            pltpu.VMEM((slots + 1, rows, rows), BF16),
            pltpu.VMEM((SPAN, rows, members * rows), BF16),
            pltpu.VMEM((2, members // 2, rows, SPAN * rows), BF16),
            pltpu.VMEM((2, members, rows, half), BF16),
            pltpu.VMEM((2, SPAN, rows, half), BF16),
            pltpu.VMEM((2, SPAN, rows, half), BF16),
            pltpu.VMEM((2, SPAN, rows, half), BF16),
            pltpu.VMEM((flows, rows, half), BF16),
            pltpu.VMEM((flows, rows, half), BF16),
            pltpu.VMEM((4, rows, half), BF16),
            pltpu.VMEM((4, rows, half), BF16),
            pltpu.VMEM((2, 2, members // 2, rows, half), F32),
            pltpu.VMEM((feat, feat), BF16),
            pltpu.VMEM((feat, feat), BF16),
            pltpu.VMEM((rows, feat), F32),
            pltpu.VMEM((rows, feat), F32),
            dma((11,)),
            dma(()),
            dma((flows,)),
            dma((flows,)),
            dma((4,)),
            dma((4,)),
            dma((2 * SPAN,)),
            dma((2 * SPAN,)),
            dma((12,)),
            dma((12,)),
            dma((flows,)),
            dma((flows,)),
            dma((4,)),
            dma((4,)),
        ],
        compiler_params=pltpu.CompilerParams(
            collective_id=0, has_side_effects=True, vmem_limit_bytes=56 * 1024 * 1024
        ),
    )(
        dest_block,
        col_tile,
        tile_count,
        node_feats,
        edge_tiles,
        w_self,
        w_agg,
        in_bias[None],
        w_out,
        out_gain[None],
        grad_out,
    )
    return pl.pallas_call(
        deliver,
        out_shape=results,
        in_specs=[in_vmem] * 3,
        out_specs=[anywhere] * 3,
        scratch_shapes=[dma((6,))],
        compiler_params=pltpu.CompilerParams(vmem_limit_bytes=56 * 1024 * 1024),
    )(*[pltpu.with_memory_space_constraint(one, pltpu.VMEM) for one in made])


def solution(mesh):
    shards = ("blk", "grp")
    return jax.shard_map(
        body,
        mesh=mesh,
        in_specs=(
            P(shards, None),
            P(shards, None),
            P(shards, None),
            P(shards),
            P(shards, None, None, None),
            P(),
            P(),
            P(),
            P(),
            P(),
            P(shards, None),
        ),
        out_specs=(P(shards, None), P(shards, None), P(shards, None, None, None)),
        check_vma=False,
    )
```
